32 devices in a mesh: groups: 2 (over y), patch: 4 (over z), fsdp: 2 (over x), sub: 2 (over core).
Axes of the slice: x: 2, y: 2, z: 4, core: 2. Of those that a mesh axis runs over, the one named last changes fastest.
Arguments:
- noisy_field: float32 [128, 512], P(('groups', 'patch'), 'sub'), parts along dimension 0, may hold values from -6 to 6
- noise_draw: float32 [128, 512], P(('groups', 'patch'), 'sub'), parts along dimension 0, may hold values from -6 to 6
- cond_features: bfloat16 [128, 512, 128], P(('groups', 'patch'), 'sub'), parts along dimension 0, may hold values from -6 to 6
- sigma_now: float32 [1], replicated, may hold values from 0.5 to 2
- sigma_next: float32 [1], replicated, may hold values from 0.1 to 0.4
- field_proj: float32 [128], replicated, may hold values from -6 to 6
- fine_kernels: bfloat16 [2, 9, 128, 128], replicated, may hold values from -0.1875 to 0.1875
- coarse_kernel: bfloat16 [9, 256, 256], replicated, may hold values from -0.125 to 0.125
- down_proj: bfloat16 [128, 256], replicated, may hold values from -0.5 to 0.5
- up_proj: bfloat16 [256, 128], replicated, may hold values from -0.375 to 0.375
- out_proj: bfloat16 [128], replicated, may hold values from -0.5 to 0.5
Outputs:
- next_field: float32 [128, 512], P(('groups', 'patch'), 'sub'), parts along dimension 0
The draws below stay inside these ranges and needn't reach their ends.
There are 2 independent parts, one for each index of `groups`. The reference program is written for one: setup_inputs(seed, part) draws one part's arguments, and reference() takes and returns one part's arrays. A program takes and returns all parts, laid end to end along the dimension named above; an argument that names none is the same for every part. Nothing has to cross between parts.
All inputs are finite; a program needn't handle non-finite values.
Results may differ from the reference program's by a relative error of at most 0.008.
Values may be sent and summed in bfloat16 or wider, within the bound.
A program may use at most 64 MiB of HBM per device.

```python
import math
import jax
import jax.numpy as jnp
from jax import lax

C1 = 128
C2 = 256
NR = 64
NC = 512


def shard_levels(rng, extent, pieces, smallest, high):
    loudness = 1.0
    for axis_at, blocks in pieces:
        heights = jax.random.uniform(jax.random.fold_in(jax.random.fold_in(rng, 6), axis_at), (blocks,), jnp.float32, smallest / len(pieces), high / len(pieces))
        loudness = loudness * jnp.repeat(jnp.exp(heights), extent[axis_at] // blocks).reshape((-1,) + (1,) * (len(extent) - 1 - axis_at))
    return loudness


def noise(own_key, shape, width, reach, split=(), kind=jnp.bfloat16):
    entries = width * jax.random.normal(own_key, shape, jnp.float32)
    if split:
        entries = entries * shard_levels(own_key, shape, split, -0.22, 0.18)
    return jnp.clip(entries, -reach, reach).astype(kind)


def setup_inputs(seed: int = 0, part: int = 0) -> dict:
    key_of = jax.random.split(jax.random.key(seed), 12)
    part_splits = jax.random.split(jax.random.fold_in(key_of[11], part), 12)
    return {
        "noisy_field": noise(part_splits[0], (NR, NC), 1.0, 6.0, ((0, 4), (1, 2)), jnp.float32),
        "noise_draw": noise(part_splits[1], (NR, NC), 1.0, 6.0, ((0, 4), (1, 2)), jnp.float32),
        "cond_features": noise(part_splits[2], (NR, NC, C1), 1.0, 6.0, ((0, 4), (1, 2))),
        "sigma_now": jnp.clip(jnp.exp(jax.random.uniform(key_of[3], (1,), jnp.float32, math.log(0.5), math.log(2.0))), 0.5, 2.0),
        "sigma_next": jnp.clip(jnp.exp(jax.random.uniform(key_of[4], (1,), jnp.float32, math.log(0.1), math.log(0.4))), 0.1, 0.4),
        "field_proj": noise(key_of[5], (C1,), 1 ** -0.5, 6.0, (), jnp.float32),
        "fine_kernels": noise(key_of[6], (2, 9, C1, C1), (9 * C1) ** -0.5, 0.1875),
        "coarse_kernel": noise(key_of[7], (9, C2, C2), (9 * C2) ** -0.5, 0.125),
        "down_proj": noise(key_of[8], (C1, C2), C1 ** -0.5, 0.5),
        "up_proj": noise(key_of[9], (C2, C1), C2 ** -0.5, 0.375),
        "out_proj": noise(key_of[10], (C1,), C1 ** -0.5, 0.5),
    }


def conv_full(values, kernel):
    height = values.shape[0]
    breadth = values.shape[1]
    channels = values.shape[2]
    padded = jnp.pad(values, ((1, 1), (1, 1), (0, 0)))
    summed = jnp.zeros((height * breadth, kernel.shape[2]), jnp.float32)
    for kernel_tap in range(9):
        row_off = kernel_tap // 3
        col_off = kernel_tap % 3
        window = padded[row_off:row_off + height, col_off:col_off + breadth, :].reshape(height * breadth, channels)
        summed = summed + jnp.dot(window, kernel[kernel_tap], preferred_element_type=jnp.float32)
    return summed.reshape(height, breadth, kernel.shape[2])

def reference(noisy_field, noise_draw, cond_features, sigma_now, sigma_next, field_proj, fine_kernels, coarse_kernel, down_proj, up_proj, out_proj):
    height = noisy_field.shape[0]
    breadth = noisy_field.shape[1]
    level_now = sigma_now[0]
    level_next = sigma_next[0]
    scale_in = 1.0 / jnp.sqrt(level_now * level_now + 1.0)
    scale_skip = 1.0 / (level_now * level_now + 1.0)
    scale_out = level_now * scale_in
    hidden0 = (cond_features.astype(jnp.float32) + (scale_in * noisy_field)[:, :, None] * field_proj).astype(jnp.bfloat16)
    hidden1 = (hidden0.astype(jnp.float32) + jax.nn.silu(conv_full(hidden0, fine_kernels[0]))).astype(jnp.bfloat16)
    pooled = hidden1.astype(jnp.float32).reshape(height // 2, 2, breadth // 2, 2, C1).mean(axis=(1, 3)).astype(jnp.bfloat16)
    coarse_in = jnp.dot(pooled.reshape(-1, C1), down_proj, preferred_element_type=jnp.float32).astype(jnp.bfloat16).reshape(height // 2, breadth // 2, C2)
    coarse_out = (coarse_in.astype(jnp.float32) + jax.nn.silu(conv_full(coarse_in, coarse_kernel))).astype(jnp.bfloat16)
    lifted = jnp.dot(coarse_out.reshape(-1, C2), up_proj, preferred_element_type=jnp.float32).reshape(height // 2, breadth // 2, C1)
    lifted = jnp.repeat(jnp.repeat(lifted, 2, axis=0), 2, axis=1)
    hidden2 = (hidden1.astype(jnp.float32) + lifted).astype(jnp.bfloat16)
    hidden3 = (hidden2.astype(jnp.float32) + jax.nn.silu(conv_full(hidden2, fine_kernels[1]))).astype(jnp.bfloat16)
    network = lax.optimization_barrier(jnp.sum(hidden3.astype(jnp.float32) * out_proj.astype(jnp.float32), axis=2))
    denoised = scale_skip * noisy_field + scale_out * network
    ratio = level_next / level_now
    spread = jnp.sqrt(level_now * level_now - level_next * level_next)
    return denoised + ratio * (noisy_field - denoised) + spread * noise_draw
```

```python
import functools
import jax
import jax.numpy as jnp
from jax import lax
from jax.experimental import pallas as pl
from jax.experimental.pallas import tpu as pltpu
from jax.sharding import PartitionSpec as P

MESH = pl.DeviceIdType.MESH
BF16 = jnp.bfloat16
F32 = jnp.float32

WAYS = ((-1, 0), (1, 0), (0, -1), (0, 1), (-1, -1), (-1, 1), (1, -1), (1, 1))
BACK = (1, 0, 3, 2, 7, 6, 5, 4)


def silu(v):
    return (0.5 * v) * (1.0 + jnp.tanh(0.5 * v))


def dot(a, b):
    return jnp.dot(a, b, preferred_element_type=F32)


def kernel(
    sizes,
    now_ref, next_ref, noisy_ref, draw_ref, proj_ref, outp_ref, down_ref, up_ref,
    cond_hbm, fine_hbm, coarse_hbm,
    out_ref,
    cond, wf, wc, x3, c3, h1, noisy_t, net,
    rows_out0, rows_in0, side_out0, side_in0, corner_out0, corner_in0,
    rows_out1, rows_in1, side_out1, side_in1, corner_out1, corner_in1,
    rows_out2, rows_in2, side_out2, side_in2, corner_out2, corner_in2,
    load_sem, send_sem, recv_sem, net_send, net_recv,
):
    n_patch, n_rep, n_sub = sizes
    n_part = n_rep * n_sub
    height, cols, c1 = cond.shape
    pairs = height // 2
    half = cols // 2
    c2 = wc.shape[2]

    p = lax.axis_index("patch")
    f = lax.axis_index("fsdp")
    s = lax.axis_index("sub")

    def place(rep, sub):
        return rep + lax.rem(sub, 2) * (n_rep - 1 - 2 * rep)

    g = place(f, s)
    q = s * n_rep + g

    def device(way):
        dp, dq = WAYS[way]
        to_p = lax.rem(p + dp + n_patch, n_patch)
        to_q = lax.rem(q + dq + n_part, n_part)
        to_s = lax.div(to_q, n_rep)
        to_f = place(lax.rem(to_q, n_rep), to_s)
        return {"patch": to_p, "fsdp": to_f, "sub": to_s}

    def has(way):
        dp, dq = WAYS[way]
        conds = []
        if dp < 0:
            conds.append(p > 0)
        if dp > 0:
            conds.append(p < n_patch - 1)
        if dq < 0:
            conds.append(q > 0)
        if dq > 0:
            conds.append(q < n_part - 1)
        both = conds[0]
        for more in conds[1:]:
            both = jnp.logical_and(both, more)
        return both

    barrier = pltpu.get_barrier_semaphore()
    greeted = n_rep - 1
    for way in range(8):
        there = has(way)

        @pl.when(there)
        def _(way=way):
            pl.semaphore_signal(barrier, inc=1, device_id=device(way), device_id_type=MESH)

        greeted = greeted + there.astype(jnp.int32)
    for step in range(1, n_rep):
        pl.semaphore_signal(
            barrier, inc=1, device_id={"fsdp": lax.rem(f + step, n_rep)}, device_id_type=MESH
        )

    first = pl.multiple_of(g * cols, cols)
    load_cond = pltpu.make_async_copy(cond_hbm.at[:, pl.ds(first, cols), :], cond, load_sem.at[0])
    load_cond.start()
    wf[:, 9:12, :, 0:c1] = jnp.zeros((2, 3, c1, c1), BF16)
    wf[:, 0:3, :, c1 : 2 * c1] = jnp.zeros((2, 3, c1, c1), BF16)
    load_fine = []
    load_coarse = pltpu.make_async_copy(coarse_hbm, wc, load_sem.at[1])
    for layer in range(2):
        load_fine.append(
            [
                pltpu.make_async_copy(
                    fine_hbm.at[layer], wf.at[layer, 0:9, :, 0:c1], load_sem.at[2 + 2 * layer]
                ),
                pltpu.make_async_copy(
                    fine_hbm.at[layer], wf.at[layer, 3:12, :, c1 : 2 * c1], load_sem.at[3 + 2 * layer]
                ),
            ]
        )
    for copy in load_fine[0] + [load_coarse] + load_fine[1]:
        copy.start()

    def copies(level, rows_out, rows_in, side_out, side_in, corner_out, corner_in):
        routes = [
            (rows_out.at[0], rows_in.at[1]),
            (rows_out.at[1], rows_in.at[0]),
            (side_out.at[0], side_in.at[1]),
            (side_out.at[1], side_in.at[0]),
        ] + [(corner_out.at[k], corner_in.at[k]) for k in range(4)]

        def copy(way):
            return pltpu.make_async_remote_copy(
                src_ref=routes[way][0],
                dst_ref=routes[way][1],
                send_sem=send_sem.at[level, way],
                recv_sem=recv_sem.at[level, way],
                device_id=device(way),
                device_id_type=MESH,
            )

        def clear():
            for way in range(8):
                @pl.when(jnp.logical_not(has(BACK[way])))
                def _(way=way):
                    into = routes[way][1]
                    into[...] = jnp.zeros(into.shape, into.dtype)

        def send(ways):
            for way in ways:
                @pl.when(has(way))
                def _(way=way):
                    copy(way).start()

        def receive(ways):
            for way in ways:
                @pl.when(has(BACK[way]))
                def _(way=way):
                    copy(way).wait_recv()

        def finish():
            for way in range(8):
                @pl.when(has(way))
                def _(way=way):
                    copy(way).wait_send()

        return clear, send, receive, finish

    bufs = (
        (rows_out0, rows_in0, side_out0, side_in0, corner_out0, corner_in0),
        (rows_out1, rows_in1, side_out1, side_in1, corner_out1, corner_in1),
        (rows_out2, rows_in2, side_out2, side_in2, corner_out2, corner_in2),
    )
    links = [copies(level, *bufs[level]) for level in range(3)]
    for clear, _, _, _ in links:
        clear()

    def put_row(level, wide, row, count, value):
        rows_out, _, side_out, _, corner_out, _ = bufs[level]
        length, depth = value.shape
        x = value.astype(F32)
        wide[row + 1, :, 0:depth] = pltpu.roll(x, 1, axis=0).astype(BF16)
        wide[row + 1, :, depth : 2 * depth] = value
        wide[row + 1, :, 2 * depth : 3 * depth] = pltpu.roll(x, length - 1, axis=0).astype(BF16)
        left = x[0:1, :]
        right = x[length - 1 : length, :]
        side_out[0, row : row + 1, :] = left
        side_out[1, row : row + 1, :] = right
        for end, at in ((0, 0), (1, count - 1)):
            if row == at:
                rows_out[end] = value
                corner_out[2 * end] = jnp.broadcast_to(left, (8, depth))
                corner_out[2 * end + 1] = jnp.broadcast_to(right, (8, depth))

    def patch_sides(level, wide, count):
        side_in = bufs[level][3]
        length = wide.shape[1]
        depth = wide.shape[2] // 3
        at = lax.broadcasted_iota(jnp.int32, (16, depth), 0)

        def body(row, carry):
            head = wide[row + 1, 0:16, 0:depth].astype(F32)
            head = jnp.where(at == 0, side_in[0, pl.ds(row, 1), :], head)
            wide[row + 1, 0:16, 0:depth] = head.astype(BF16)
            tail = wide[row + 1, length - 16 : length, 2 * depth :].astype(F32)
            tail = jnp.where(at == 15, side_in[1, pl.ds(row, 1), :], tail)
            wide[row + 1, length - 16 : length, 2 * depth :] = tail.astype(BF16)
            return carry

        lax.fori_loop(0, count, body, 0, unroll=True)

    def put_halo(level, wide, count):
        _, rows_in, _, _, _, corner_in = bufs[level]
        length = wide.shape[1]
        depth = wide.shape[2] // 3
        at = lax.broadcasted_iota(jnp.int32, (length, depth), 0)
        for end, row, left, right in ((0, 0, 3, 2), (1, count + 1, 1, 0)):
            value = rows_in[end]
            x = value.astype(F32)
            before = jnp.where(at == 0, corner_in[left, 0:1, :], pltpu.roll(x, 1, axis=0))
            after = jnp.where(
                at == length - 1, corner_in[right, 0:1, :], pltpu.roll(x, length - 1, axis=0)
            )
            wide[row, :, 0:depth] = before.astype(BF16)
            wide[row, :, depth : 2 * depth] = value
            wide[row, :, 2 * depth : 3 * depth] = after.astype(BF16)

    level_now = jnp.full((1, c1), now_ref[0], F32)
    scale_in = 1.0 / jnp.sqrt(level_now * level_now + 1.0)
    scale_one = scale_in[0:1, 0:1]
    noisy_t[...] = jnp.transpose(scale_one * noisy_ref[...])
    mine = noisy_t[pl.ds(first, cols), :]
    proj = proj_ref[...]
    load_cond.wait()
    for row in range(height):
        value = cond[row].astype(F32) + mine[:, row : row + 1] * proj
        put_row(0, x3, row, height, value.astype(BF16))
    pl.semaphore_wait(barrier, greeted)
    links[0][1]((2, 3, 0, 1, 4, 5, 6, 7))

    def fine_sum(layer, group):
        lhs = jnp.concatenate(
            [jnp.concatenate([x3[2 * i + j] for j in range(4)], axis=1) for i in group], axis=0
        )
        return dot(lhs, wf[layer].reshape(12 * c1, 2 * c1))

    inner = list(range(1, pairs - 1))
    groups = [inner[k : k + 2] for k in range(0, len(inner), 2)]
    border = sorted({0, pairs - 1})

    pool_at = lax.broadcasted_iota(jnp.int32, (half, 2 * cols), 1)
    pool_to = lax.broadcasted_iota(jnp.int32, (half, 2 * cols), 0)
    pool_at = jnp.where(pool_at >= cols, pool_at - cols, pool_at)
    pool = jnp.where(jnp.right_shift(pool_at, 1) == pool_to, 0.25, 0.0).astype(BF16)

    def first_conv(group):
        acc = fine_sum(0, group)
        pooled = []
        for k, i in enumerate(group):
            both = []
            for j in range(2):
                row = 2 * i + j
                centre = x3[row + 1, :, c1 : 2 * c1].astype(F32)
                part = acc[k * cols : (k + 1) * cols, j * c1 : (j + 1) * c1]
                value = (centre + silu(part)).astype(BF16)
                h1[row] = value
                both.append(value)
            pooled.append(dot(pool, jnp.concatenate(both, axis=0)).astype(BF16))
        lower = dot(jnp.concatenate(pooled, axis=0), down_ref[...]).astype(BF16)
        for k, i in enumerate(group):
            put_row(1, c3, i, pairs, lower[k * half : (k + 1) * half])

    links[0][2]((2, 3))
    patch_sides(0, x3, height)
    for copy in load_fine[0]:
        copy.wait()
    for group in groups:
        first_conv(group)
    links[0][2]((0, 1, 4, 5, 6, 7))
    put_halo(0, x3, height)
    first_conv(border)
    links[1][1]((2, 3, 0, 1, 4, 5, 6, 7))

    lift_at = lax.broadcasted_iota(jnp.int32, (cols, half), 0)
    lift_to = lax.broadcasted_iota(jnp.int32, (cols, half), 1)
    lift = jnp.where(jnp.right_shift(lift_at, 1) == lift_to, 1.0, 0.0).astype(BF16)

    def coarse_conv(group):
        lhs = jnp.concatenate(
            [jnp.concatenate([c3[i + j] for j in range(3)], axis=1) for i in group], axis=0
        )
        acc = dot(lhs, wc[...].reshape(9 * c2, c2))
        wide = []
        for k, i in enumerate(group):
            centre = c3[i + 1, :, c2 : 2 * c2].astype(F32)
            value = (centre + silu(acc[k * half : (k + 1) * half])).astype(BF16)
            wide.append(dot(lift, value).astype(BF16))
        lifted = dot(jnp.concatenate(wide, axis=0), up_ref[...])
        for k, i in enumerate(group):
            for j in range(2):
                row = 2 * i + j
                value = h1[row].astype(F32) + lifted[k * cols : (k + 1) * cols]
                put_row(2, x3, row, height, value.astype(BF16))

    links[1][2]((2, 3))
    patch_sides(1, c3, pairs)
    load_coarse.wait()
    coarse_conv(inner)
    links[1][2]((0, 1, 4, 5, 6, 7))
    put_halo(1, c3, pairs)
    coarse_conv(border)
    links[2][1]((2, 3, 0, 1, 4, 5, 6, 7))

    outp = jnp.broadcast_to(outp_ref[...].astype(F32), (16, c1)).astype(BF16)

    def second_conv(group):
        acc = fine_sum(1, group)
        for k, i in enumerate(group):
            for j in range(2):
                row = 2 * i + j
                centre = x3[row + 1, :, c1 : 2 * c1].astype(F32)
                part = acc[k * cols : (k + 1) * cols, j * c1 : (j + 1) * c1]
                value = (centre + silu(part)).astype(BF16)
                total = lax.dot_general(
                    outp, value, (((1,), (1,)), ((), ())), preferred_element_type=F32
                )
                net[g, row : row + 1, :] = total[0:1, :]

    links[2][2]((2, 3))
    patch_sides(2, x3, height)
    for copy in load_fine[1]:
        copy.wait()
    for group in groups:
        second_conv(group)
    links[2][2]((0, 1, 4, 5, 6, 7))
    put_halo(2, x3, height)
    second_conv(border)

    shares = []
    for step in range(1, n_rep):
        share = pltpu.make_async_remote_copy(
            src_ref=net.at[g],
            dst_ref=net.at[g],
            send_sem=net_send.at[step - 1],
            recv_sem=net_recv.at[step - 1],
            device_id={"fsdp": lax.rem(f + step, n_rep)},
            device_id_type=MESH,
        )
        share.start()
        shares.append(share)
    for _, _, _, finish in links:
        finish()
    for step in range(1, n_rep):
        owner = place(lax.rem(f + n_rep - step, n_rep), s)
        pltpu.make_async_remote_copy(
            src_ref=net.at[owner],
            dst_ref=net.at[owner],
            send_sem=net_send.at[step - 1],
            recv_sem=net_recv.at[step - 1],
            device_id={"fsdp": lax.rem(f + step, n_rep)},
            device_id_type=MESH,
        ).wait_recv()
    for share in shares:
        share.wait_send()

    network = jnp.concatenate([net[k] for k in range(n_rep)], axis=1)
    level_next = jnp.full((1, c1), next_ref[0], F32)
    scale_skip = (1.0 / (level_now * level_now + 1.0))[0:1, 0:1]
    scale_out = (level_now * scale_in)[0:1, 0:1]
    ratio = (level_next / level_now)[0:1, 0:1]
    spread = jnp.sqrt(level_now * level_now - level_next * level_next)[0:1, 0:1]
    noisy = noisy_ref[...]
    denoised = scale_skip * noisy + scale_out * network
    out_ref[...] = denoised + ratio * (noisy - denoised) + spread * draw_ref[...]


def per_device(
    sizes,
    noisy_field, noise_draw, cond_features, sigma_now, sigma_next, field_proj,
    fine_kernels, coarse_kernel, down_proj, up_proj, out_proj,
):
    n_rep = sizes[1]
    height, breadth, c1 = cond_features.shape
    c2 = coarse_kernel.shape[2]
    cols = breadth // n_rep
    pairs, half = height // 2, cols // 2

    def level_bufs(rows, length, depth):
        return [
            pltpu.VMEM((2, length, depth), BF16),
            pltpu.VMEM((2, length, depth), BF16),
            pltpu.VMEM((2, rows, depth), F32),
            pltpu.VMEM((2, rows, depth), F32),
            pltpu.VMEM((4, 8, depth), F32),
            pltpu.VMEM((4, 8, depth), F32),
        ]

    smem = pl.BlockSpec(memory_space=pltpu.SMEM)
    vmem = pl.BlockSpec(memory_space=pltpu.VMEM)
    hbm = pl.BlockSpec(memory_space=pl.ANY)
    return pl.pallas_call(
        functools.partial(kernel, sizes),
        out_shape=jax.ShapeDtypeStruct((height, breadth), F32),
        in_specs=[smem] * 2 + [vmem] * 6 + [hbm] * 3,
        out_specs=vmem,
        scratch_shapes=[
            pltpu.VMEM((height, cols, c1), BF16),
            pltpu.VMEM((2, 12, c1, 2 * c1), BF16),
            pltpu.VMEM((9, c2, c2), BF16),
            pltpu.VMEM((height + 2, cols, 3 * c1), BF16),
            pltpu.VMEM((pairs + 2, half, 3 * c2), BF16),
            pltpu.VMEM((height, cols, c1), BF16),
            pltpu.VMEM((breadth, height), F32),
            pltpu.VMEM((n_rep, height, cols), F32),
        ]
        + level_bufs(height, cols, c1)
        + level_bufs(pairs, half, c2)
        + level_bufs(height, cols, c1)
        + [
            pltpu.SemaphoreType.DMA((6,)),
            pltpu.SemaphoreType.DMA((3, 8)),
            pltpu.SemaphoreType.DMA((3, 8)),
            pltpu.SemaphoreType.DMA((max(n_rep - 1, 1),)),
            pltpu.SemaphoreType.DMA((max(n_rep - 1, 1),)),
        ],
        compiler_params=pltpu.CompilerParams(
            collective_id=0, has_side_effects=True, vmem_limit_bytes=48 * 1024 * 1024
        ),
    )(
        sigma_now, sigma_next, noisy_field, noise_draw,
        field_proj.reshape(1, c1), out_proj.reshape(1, c1), down_proj, up_proj,
        cond_features, fine_kernels, coarse_kernel,
    )


def solution(mesh):
    sizes = (mesh.shape["patch"], mesh.shape["fsdp"], mesh.shape["sub"])
    field = P(("groups", "patch"), "sub")
    return jax.shard_map(
        functools.partial(per_device, sizes),
        mesh=mesh,
        in_specs=(field, field, P(("groups", "patch"), "sub", None)) + (P(),) * 8,
        out_specs=field,
        check_vma=False,
    )
```

```python
import functools
import jax
import jax.numpy as jnp
from jax import lax
from jax.experimental import pallas as pl
from jax.experimental.pallas import tpu as pltpu
from jax.sharding import PartitionSpec as P

MESH = pl.DeviceIdType.MESH
BF16 = jnp.bfloat16
F32 = jnp.float32

WAYS = ((-1, 0), (1, 0), (0, -1), (0, 1), (-1, -1), (-1, 1), (1, -1), (1, 1))
BACK = (1, 0, 3, 2, 7, 6, 5, 4)


def silu(v):
    return (0.5 * v) * (1.0 + jnp.tanh(0.5 * v))


def dot(a, b):
    return jnp.dot(a, b, preferred_element_type=F32)


def kernel(
    sizes,
    now_ref, next_ref, noisy_hbm, draw_hbm, proj_hbm, outp_hbm, down_hbm, up_hbm,
    cond_hbm, fine_hbm, coarse_hbm,
    out_ref,
    noisy_ref, draw_ref, proj_ref, outp_ref, down_ref, up_ref,
    cond, wf, wc, x3, c3, h1, noisy_t, lifts, net,
    rows_out0, rows_in0, side_out0, side_in0, corner_out0, corner_in0,
    rows_out1, rows_in1, side_out1, side_in1, corner_out1, corner_in1,
    rows_out2, rows_in2, side_out2, side_in2, corner_out2, corner_in2,
    load_sem, send_sem, recv_sem, net_send, net_recv,
):
    n_patch, n_rep, n_sub = sizes
    n_part = n_rep * n_sub
    height, cols, c1 = cond.shape
    pairs = height // 2
    half = cols // 2
    c2 = wc.shape[2]

    p = lax.axis_index("patch")
    f = lax.axis_index("fsdp")
    s = lax.axis_index("sub")

    def place(rep, sub):
        return rep + lax.rem(sub, 2) * (n_rep - 1 - 2 * rep)

    g = place(f, s)
    q = s * n_rep + g

    def device(way):
        dp, dq = WAYS[way]
        to_p = lax.rem(p + dp + n_patch, n_patch)
        to_q = lax.rem(q + dq + n_part, n_part)
        to_s = lax.div(to_q, n_rep)
        to_f = place(lax.rem(to_q, n_rep), to_s)
        return {"patch": to_p, "fsdp": to_f, "sub": to_s}

    def has(way):
        dp, dq = WAYS[way]
        conds = []
        if dp < 0:
            conds.append(p > 0)
        if dp > 0:
            conds.append(p < n_patch - 1)
        if dq < 0:
            conds.append(q > 0)
        if dq > 0:
            conds.append(q < n_part - 1)
        both = conds[0]
        for more in conds[1:]:
            both = jnp.logical_and(both, more)
        return both

    barrier = pltpu.get_barrier_semaphore()
    greeted = n_rep - 1
    for way in range(8):
        there = has(way)

        @pl.when(there)
        def _(way=way):
            pl.semaphore_signal(barrier, inc=1, device_id=device(way), device_id_type=MESH)

        greeted = greeted + there.astype(jnp.int32)
    for step in range(1, n_rep):
        pl.semaphore_signal(
            barrier, inc=1, device_id={"fsdp": lax.rem(f + step, n_rep)}, device_id_type=MESH
        )

    first = pl.multiple_of(g * cols, cols)
    load_cond = pltpu.make_async_copy(cond_hbm.at[:, pl.ds(first, cols), :], cond, load_sem.at[0])
    load_small = [
        pltpu.make_async_copy(src, dst, load_sem.at[6 + k])
        for k, (src, dst) in enumerate(
            (
                (noisy_hbm, noisy_ref),
                (proj_hbm, proj_ref),
                (down_hbm, down_ref),
                (up_hbm, up_ref),
                (outp_hbm, outp_ref),
                (draw_hbm, draw_ref),
            )
        )
    ]
    load_small[0].start()
    load_small[1].start()
    load_cond.start()
    wf[:, 9:12, :, 0:c1] = jnp.zeros((2, 3, c1, c1), BF16)
    wf[:, 0:3, :, c1 : 2 * c1] = jnp.zeros((2, 3, c1, c1), BF16)
    load_fine = []
    load_coarse = pltpu.make_async_copy(coarse_hbm, wc, load_sem.at[1])
    for layer in range(2):
        load_fine.append(
            [
                pltpu.make_async_copy(
                    fine_hbm.at[layer], wf.at[layer, 0:9, :, 0:c1], load_sem.at[2 + 2 * layer]
                ),
                pltpu.make_async_copy(
                    fine_hbm.at[layer], wf.at[layer, 3:12, :, c1 : 2 * c1], load_sem.at[3 + 2 * layer]
                ),
            ]
        )
    for copy in load_fine[0] + [load_small[2], load_coarse, load_small[3]] + load_fine[1]:
        copy.start()
    load_small[4].start()
    load_small[5].start()

    def copies(level, rows_out, rows_in, side_out, side_in, corner_out, corner_in):
        routes = [
            (rows_out.at[0], rows_in.at[1]),
            (rows_out.at[1], rows_in.at[0]),
            (side_out.at[0], side_in.at[1]),
            (side_out.at[1], side_in.at[0]),
        ] + [(corner_out.at[k], corner_in.at[k]) for k in range(4)]

        def copy(way):
            return pltpu.make_async_remote_copy(
                src_ref=routes[way][0],
                dst_ref=routes[way][1],
                send_sem=send_sem.at[level, way],
                recv_sem=recv_sem.at[level, way],
                device_id=device(way),
                device_id_type=MESH,
            )

        def clear():
            for way in range(8):
                @pl.when(jnp.logical_not(has(BACK[way])))
                def _(way=way):
                    into = routes[way][1]
                    into[...] = jnp.zeros(into.shape, into.dtype)

        def send(ways):
            for way in ways:
                @pl.when(has(way))
                def _(way=way):
                    copy(way).start()

        def receive(ways):
            for way in ways:
                @pl.when(has(BACK[way]))
                def _(way=way):
                    copy(way).wait_recv()

        def finish():
            for way in range(8):
                @pl.when(has(way))
                def _(way=way):
                    copy(way).wait_send()

        return clear, send, receive, finish

    bufs = (
        (rows_out0, rows_in0, side_out0, side_in0, corner_out0, corner_in0),
        (rows_out1, rows_in1, side_out1, side_in1, corner_out1, corner_in1),
        (rows_out2, rows_in2, side_out2, side_in2, corner_out2, corner_in2),
    )
    links = [copies(level, *bufs[level]) for level in range(3)]
    for clear, _, _, _ in links:
        clear()

    def put_row(level, wide, row, value):
        side_out = bufs[level][2]
        length, depth = value.shape
        x = value.astype(F32)
        wide[row + 1, :, 0:depth] = pltpu.roll(x, 1, axis=0).astype(BF16)
        wide[row + 1, :, depth : 2 * depth] = value
        wide[row + 1, :, 2 * depth : 3 * depth] = pltpu.roll(x, length - 1, axis=0).astype(BF16)
        side_out[0, pl.ds(row, 1), :] = x[0:1, :]
        side_out[1, pl.ds(row, 1), :] = x[length - 1 : length, :]

    def put_ends(level, wide, count):
        rows_out, _, side_out, _, corner_out, _ = bufs[level]
        depth = wide.shape[2] // 3
        for end, row in ((0, 0), (1, count - 1)):
            rows_out[end] = wide[row + 1, :, depth : 2 * depth]
            for side in range(2):
                corner_out[2 * end + side] = jnp.broadcast_to(
                    side_out[side, row : row + 1, :], (8, depth)
                )

    def patch_sides(level, wide, count):
        side_in = bufs[level][3]
        length = wide.shape[1]
        depth = wide.shape[2] // 3
        at = lax.broadcasted_iota(jnp.int32, (16, depth), 0)

        def body(row, carry):
            head = wide[row + 1, 0:16, 0:depth].astype(F32)
            head = jnp.where(at == 0, side_in[0, pl.ds(row, 1), :], head)
            wide[row + 1, 0:16, 0:depth] = head.astype(BF16)
            tail = wide[row + 1, length - 16 : length, 2 * depth :].astype(F32)
            tail = jnp.where(at == 15, side_in[1, pl.ds(row, 1), :], tail)
            wide[row + 1, length - 16 : length, 2 * depth :] = tail.astype(BF16)
            return carry

        lax.fori_loop(0, count, body, 0)

    def put_halo(level, wide, count):
        _, rows_in, _, _, _, corner_in = bufs[level]
        length = wide.shape[1]
        depth = wide.shape[2] // 3
        at = lax.broadcasted_iota(jnp.int32, (length, depth), 0)
        for end, row, left, right in ((0, 0, 3, 2), (1, count + 1, 1, 0)):
            value = rows_in[end]
            x = value.astype(F32)
            before = jnp.where(at == 0, corner_in[left, 0:1, :], pltpu.roll(x, 1, axis=0))
            after = jnp.where(
                at == length - 1, corner_in[right, 0:1, :], pltpu.roll(x, length - 1, axis=0)
            )
            wide[row, :, 0:depth] = before.astype(BF16)
            wide[row, :, depth : 2 * depth] = value
            wide[row, :, 2 * depth : 3 * depth] = after.astype(BF16)

    level_now = jnp.full((1, c1), now_ref[0], F32)
    scale_in = 1.0 / jnp.sqrt(level_now * level_now + 1.0)
    scale_one = scale_in[0:1, 0:1]
    load_small[0].wait()
    noisy_t[...] = jnp.transpose(scale_one * noisy_ref[...])
    mine = noisy_t[pl.ds(first, cols), :]
    load_small[1].wait()
    proj = proj_ref[...]
    load_cond.wait()
    for row in range(height):
        value = cond[row].astype(F32) + mine[:, row : row + 1] * proj
        cond[row] = value.astype(BF16)

    def spread_row(row, carry):
        put_row(0, x3, row, cond[row])
        return carry

    lax.fori_loop(0, height, spread_row, 0)
    put_ends(0, x3, height)
    pl.semaphore_wait(barrier, greeted)
    links[0][1]((2, 3, 0, 1, 4, 5, 6, 7))

    def fine_sum(layer, group):
        lhs = jnp.concatenate(
            [jnp.concatenate([x3[2 * i + j] for j in range(4)], axis=1) for i in group], axis=0
        )
        return dot(lhs, wf[layer].reshape(12 * c1, 2 * c1))

    inner = list(range(1, pairs - 1))
    border = [0, pairs - 1]
    n_steps = pairs // 2

    def over_pairs(conv, before_border):
        def body(step, carry):
            last = step == n_steps - 1

            @pl.when(last)
            def _():
                before_border()

            low = lax.rem(1 + 2 * step, pairs - 1)
            high = low + 1 + (pairs - 2) * lax.div(step, n_steps - 1)
            conv((low, high))
            return carry

        lax.fori_loop(0, n_steps, body, 0)

    pool_at = lax.broadcasted_iota(jnp.int32, (half, 2 * cols), 1)
    pool_to = lax.broadcasted_iota(jnp.int32, (half, 2 * cols), 0)
    pool_at = jnp.where(pool_at >= cols, pool_at - cols, pool_at)
    pool = jnp.where(jnp.right_shift(pool_at, 1) == pool_to, 0.25, 0.0).astype(BF16)

    def first_conv(group):
        acc = fine_sum(0, group)
        pooled = []
        for k, i in enumerate(group):
            both = []
            for j in range(2):
                row = 2 * i + j
                centre = x3[row + 1, :, c1 : 2 * c1].astype(F32)
                part = acc[k * cols : (k + 1) * cols, j * c1 : (j + 1) * c1]
                value = (centre + silu(part)).astype(BF16)
                h1[row] = value
                both.append(value)
            pooled.append(dot(pool, jnp.concatenate(both, axis=0)).astype(BF16))
        lower = dot(jnp.concatenate(pooled, axis=0), down_ref[...]).astype(BF16)
        for k, i in enumerate(group):
            put_row(1, c3, i, lower[k * half : (k + 1) * half])

    links[0][2]((2, 3))
    patch_sides(0, x3, height)
    for copy in load_fine[0]:
        copy.wait()
    load_small[2].wait()

    def first_halo():
        links[0][2]((0, 1, 4, 5, 6, 7))
        put_halo(0, x3, height)

    over_pairs(first_conv, first_halo)
    put_ends(1, c3, pairs)
    links[1][1]((2, 3, 0, 1, 4, 5, 6, 7))

    lift_at = lax.broadcasted_iota(jnp.int32, (cols, half), 0)
    lift_to = lax.broadcasted_iota(jnp.int32, (cols, half), 1)
    lift = jnp.where(jnp.right_shift(lift_at, 1) == lift_to, 1.0, 0.0).astype(BF16)

    def coarse_conv(group):
        lhs = jnp.concatenate(
            [jnp.concatenate([c3[i + j] for j in range(3)], axis=1) for i in group], axis=0
        )
        acc = dot(lhs, wc[...].reshape(9 * c2, c2))
        wide = []
        for k, i in enumerate(group):
            centre = c3[i + 1, :, c2 : 2 * c2].astype(F32)
            value = (centre + silu(acc[k * half : (k + 1) * half])).astype(BF16)
            wide.append(dot(lift, value).astype(BF16))
        lifted = dot(jnp.concatenate(wide, axis=0), up_ref[...])
        for k, i in enumerate(group):
            lifts[i] = lifted[k * cols : (k + 1) * cols]

    def lift_pair(i):
        lifted = lifts[i]
        for j in range(2):
            row = 2 * i + j
            put_row(2, x3, row, (h1[row].astype(F32) + lifted).astype(BF16))

    def lift_inner(i, carry):
        lift_pair(i)
        return carry

    def lift_border(k, carry):
        lift_pair(k * (pairs - 1))
        return carry

    links[1][2]((2, 3))
    patch_sides(1, c3, pairs)
    load_coarse.wait()
    load_small[3].wait()
    coarse_conv(inner)
    lax.fori_loop(1, pairs - 1, lift_inner, 0)
    links[1][2]((0, 1, 4, 5, 6, 7))
    put_halo(1, c3, pairs)
    coarse_conv(border)
    lax.fori_loop(0, 2, lift_border, 0)
    put_ends(2, x3, height)
    links[2][1]((2, 3, 0, 1, 4, 5, 6, 7))

    load_small[4].wait()
    outp = jnp.broadcast_to(outp_ref[...].astype(F32), (16, c1)).astype(BF16)

    def second_conv(group):
        acc = fine_sum(1, group)
        for k, i in enumerate(group):
            for j in range(2):
                row = 2 * i + j
                centre = x3[row + 1, :, c1 : 2 * c1].astype(F32)
                part = acc[k * cols : (k + 1) * cols, j * c1 : (j + 1) * c1]
                value = (centre + silu(part)).astype(BF16)
                total = lax.dot_general(
                    outp, value, (((1,), (1,)), ((), ())), preferred_element_type=F32
                )
                net[g, pl.ds(row, 1), :] = total[0:1, :]

    links[2][2]((2, 3))
    patch_sides(2, x3, height)
    for copy in load_fine[1]:
        copy.wait()

    def last_halo():
        links[2][2]((0, 1, 4, 5, 6, 7))
        put_halo(2, x3, height)

    over_pairs(second_conv, last_halo)

    shares = []
    for step in range(1, n_rep):
        share = pltpu.make_async_remote_copy(
            src_ref=net.at[g],
            dst_ref=net.at[g],
            send_sem=net_send.at[step - 1],
            recv_sem=net_recv.at[step - 1],
            device_id={"fsdp": lax.rem(f + step, n_rep)},
            device_id_type=MESH,
        )
        share.start()
        shares.append(share)
    for _, _, _, finish in links:
        finish()
    for step in range(1, n_rep):
        owner = place(lax.rem(f + n_rep - step, n_rep), s)
        pltpu.make_async_remote_copy(
            src_ref=net.at[owner],
            dst_ref=net.at[owner],
            send_sem=net_send.at[step - 1],
            recv_sem=net_recv.at[step - 1],
            device_id={"fsdp": lax.rem(f + step, n_rep)},
            device_id_type=MESH,
        ).wait_recv()
    for share in shares:
        share.wait_send()

    load_small[5].wait()

    network = jnp.concatenate([net[k] for k in range(n_rep)], axis=1)
    level_next = jnp.full((1, c1), next_ref[0], F32)
    scale_skip = (1.0 / (level_now * level_now + 1.0))[0:1, 0:1]
    scale_out = (level_now * scale_in)[0:1, 0:1]
    ratio = (level_next / level_now)[0:1, 0:1]
    spread = jnp.sqrt(level_now * level_now - level_next * level_next)[0:1, 0:1]
    noisy = noisy_ref[...]
    denoised = scale_skip * noisy + scale_out * network
    out_ref[...] = denoised + ratio * (noisy - denoised) + spread * draw_ref[...]


def per_device(
    sizes,
    noisy_field, noise_draw, cond_features, sigma_now, sigma_next, field_proj,
    fine_kernels, coarse_kernel, down_proj, up_proj, out_proj,
):
    n_rep = sizes[1]
    height, breadth, c1 = cond_features.shape
    c2 = coarse_kernel.shape[2]
    cols = breadth // n_rep
    pairs, half = height // 2, cols // 2

    def level_bufs(rows, length, depth):
        return [
            pltpu.VMEM((2, length, depth), BF16),
            pltpu.VMEM((2, length, depth), BF16),
            pltpu.VMEM((2, rows, depth), F32),
            pltpu.VMEM((2, rows, depth), F32),
            pltpu.VMEM((4, 8, depth), F32),
            pltpu.VMEM((4, 8, depth), F32),
        ]

    smem = pl.BlockSpec(memory_space=pltpu.SMEM)
    vmem = pl.BlockSpec(memory_space=pltpu.VMEM)
    hbm = pl.BlockSpec(memory_space=pltpu.HBM)
    return pl.pallas_call(
        functools.partial(kernel, sizes),
        out_shape=jax.ShapeDtypeStruct((height, breadth), F32),
        in_specs=[smem] * 2 + [hbm] * 9,
        out_specs=vmem,
        scratch_shapes=[
            pltpu.VMEM((height, breadth), F32),
            pltpu.VMEM((height, breadth), F32),
            pltpu.VMEM((1, c1), F32),
            pltpu.VMEM((1, c1), BF16),
            pltpu.VMEM((c1, c2), BF16),
            pltpu.VMEM((c2, c1), BF16),
            pltpu.VMEM((height, cols, c1), BF16),
            pltpu.VMEM((2, 12, c1, 2 * c1), BF16),
            pltpu.VMEM((9, c2, c2), BF16),
            pltpu.VMEM((height + 2, cols, 3 * c1), BF16),
            pltpu.VMEM((pairs + 2, half, 3 * c2), BF16),
            pltpu.VMEM((height, cols, c1), BF16),
            pltpu.VMEM((breadth, height), F32),
            pltpu.VMEM((pairs, cols, c1), F32),
            pltpu.VMEM((n_rep, height, cols), F32),
        ]
        + level_bufs(height, cols, c1)
        + level_bufs(pairs, half, c2)
        + level_bufs(height, cols, c1)
        + [
            pltpu.SemaphoreType.DMA((12,)),
            pltpu.SemaphoreType.DMA((3, 8)),
            pltpu.SemaphoreType.DMA((3, 8)),
            pltpu.SemaphoreType.DMA((max(n_rep - 1, 1),)),
            pltpu.SemaphoreType.DMA((max(n_rep - 1, 1),)),
        ],
        compiler_params=pltpu.CompilerParams(
            collective_id=0, has_side_effects=True, vmem_limit_bytes=63 * 1024 * 1024
        ),
    )(
        sigma_now, sigma_next, noisy_field, noise_draw,
        field_proj.reshape(1, c1), out_proj.reshape(1, c1), down_proj, up_proj,
        cond_features, fine_kernels, coarse_kernel,
    )


def solution(mesh):
    sizes = (mesh.shape["patch"], mesh.shape["fsdp"], mesh.shape["sub"])
    field = P(("groups", "patch"), "sub")
    return jax.shard_map(
        functools.partial(per_device, sizes),
        mesh=mesh,
        in_specs=(field, field, P(("groups", "patch"), "sub", None)) + (P(),) * 8,
        out_specs=field,
        check_vma=False,
    )
```

```python
import functools
import jax
import jax.numpy as jnp
from jax import lax
from jax.experimental import pallas as pl
from jax.experimental.pallas import tpu as pltpu
from jax.sharding import PartitionSpec as P

MESH = pl.DeviceIdType.MESH
BF16 = jnp.bfloat16
F32 = jnp.float32

WAYS = ((-1, 0), (1, 0), (0, -1), (0, 1), (-1, -1), (-1, 1), (1, -1), (1, 1))
BACK = (1, 0, 3, 2, 7, 6, 5, 4)


def silu(v):
    return (0.5 * v) * (1.0 + jnp.tanh(0.5 * v))


def dot(a, b):
    return jnp.dot(a, b, preferred_element_type=F32)


def kernel(
    sizes,
    now_ref, next_ref, noisy_hbm, draw_hbm, proj_hbm, outp_hbm, down_hbm, up_hbm,
    cond_hbm, fine_hbm, coarse_hbm,
    out_ref,
    noisy_ref, draw_ref, proj_ref, outp_ref, down_ref, up_ref,
    cond, wf, wc, hp0, hp1, hp2, h1, noisy_t, acc0, acc1, term0, term1, net,
    side_out0, side_in0, corner_out0,
    side_out1, side_in1, corner_out1,
    side_out2, side_in2, corner_out2,
    load_sem, send_sem, recv_sem, net_send, net_recv,
):
    n_patch, n_rep, n_sub = sizes
    n_part = n_rep * n_sub
    height, cols, c1 = cond.shape
    pairs = height // 2
    half = cols // 2
    c2 = wc.shape[1]

    p = lax.axis_index("patch")
    f = lax.axis_index("fsdp")
    s = lax.axis_index("sub")

    def place(rep, sub):
        return rep + lax.rem(sub, 2) * (n_rep - 1 - 2 * rep)

    g = place(f, s)
    q = s * n_rep + g

    def device(way):
        dp, dq = WAYS[way]
        to_p = lax.rem(p + dp + n_patch, n_patch)
        to_q = lax.rem(q + dq + n_part, n_part)
        to_s = lax.div(to_q, n_rep)
        to_f = place(lax.rem(to_q, n_rep), to_s)
        return {"patch": to_p, "fsdp": to_f, "sub": to_s}

    def has(way):
        dp, dq = WAYS[way]
        conds = []
        if dp < 0:
            conds.append(p > 0)
        if dp > 0:
            conds.append(p < n_patch - 1)
        if dq < 0:
            conds.append(q > 0)
        if dq > 0:
            conds.append(q < n_part - 1)
        both = conds[0]
        for more in conds[1:]:
            both = jnp.logical_and(both, more)
        return both

    barrier = pltpu.get_barrier_semaphore()
    greeted = n_rep - 1
    for way in range(8):
        there = has(way)

        @pl.when(there)
        def _(way=way):
            pl.semaphore_signal(barrier, inc=1, device_id=device(way), device_id_type=MESH)

        greeted = greeted + there.astype(jnp.int32)
    for step in range(1, n_rep):
        pl.semaphore_signal(
            barrier, inc=1, device_id={"fsdp": lax.rem(f + step, n_rep)}, device_id_type=MESH
        )

    first = pl.multiple_of(g * cols, cols)
    load_cond = pltpu.make_async_copy(cond_hbm.at[:, pl.ds(first, cols), :], cond, load_sem.at[21])
    load_small = [
        pltpu.make_async_copy(src, dst, load_sem.at[k])
        for k, (src, dst) in enumerate(
            (
                (noisy_hbm, noisy_ref),
                (proj_hbm, proj_ref),
                (down_hbm, down_ref),
                (up_hbm, up_ref),
                (outp_hbm, outp_ref),
                (draw_hbm, draw_ref),
            )
        )
    ]
    load_small[0].start()
    load_small[1].start()
    load_cond.start()
    wf[:, 3:4, :, 0 : 3 * c1] = jnp.zeros((2, 1, c1, 3 * c1), BF16)
    wf[:, 0:1, :, 3 * c1 :] = jnp.zeros((2, 1, c1, 3 * c1), BF16)
    load_fine = [
        [
            pltpu.make_async_copy(
                fine_hbm.at[layer, :, tap],
                wf.at[layer, low : low + 3, :, (3 * low + tap) * c1 : (3 * low + tap + 1) * c1],
                load_sem.at[6 + 6 * layer + 3 * low + tap],
            )
            for low in range(2)
            for tap in range(3)
        ]
        for layer in range(2)
    ]
    load_coarse = [
        pltpu.make_async_copy(
            coarse_hbm.at[:, tap], wc.at[:, :, tap * c2 : (tap + 1) * c2], load_sem.at[18 + tap]
        )
        for tap in range(3)
    ]
    for copy in load_fine[0] + [load_small[2]] + load_coarse + [load_small[3]] + load_fine[1]:
        copy.start()
    load_small[4].start()
    load_small[5].start()

    def copies(level, count, hp, side_out, side_in, corner_out):
        own = pl.ds(8, count)
        above = pl.ds(0, 8)
        below = pl.ds(count + 8, 8)
        routes = [
            (hp.at[1], hp.at[count + 1]),
            (hp.at[count], hp.at[0]),
            (side_out.at[0], side_in.at[1, own, :]),
            (side_out.at[1], side_in.at[0, own, :]),
            (corner_out.at[0], side_in.at[1, below, :]),
            (corner_out.at[1], side_in.at[0, below, :]),
            (corner_out.at[2], side_in.at[1, above, :]),
            (corner_out.at[3], side_in.at[0, above, :]),
        ]

        def copy(way):
            return pltpu.make_async_remote_copy(
                src_ref=routes[way][0],
                dst_ref=routes[way][1],
                send_sem=send_sem.at[level, way],
                recv_sem=recv_sem.at[level, way],
                device_id=device(way),
                device_id_type=MESH,
            )

        def clear():
            for way in range(8):
                @pl.when(jnp.logical_not(has(BACK[way])))
                def _(way=way):
                    into = routes[way][1]
                    into[...] = jnp.zeros(into.shape, into.dtype)

        def send(ways):
            for way in ways:
                @pl.when(has(way))
                def _(way=way):
                    copy(way).start()

        def receive(ways):
            for way in ways:
                @pl.when(has(BACK[way]))
                def _(way=way):
                    copy(way).wait_recv()

        def finish():
            for way in range(8):
                @pl.when(has(way))
                def _(way=way):
                    copy(way).wait_send()

        return clear, send, receive, finish

    bufs = (
        (height, hp0, side_out0, side_in0, corner_out0),
        (pairs, hp1, side_out1, side_in1, corner_out1),
        (height, hp2, side_out2, side_in2, corner_out2),
    )
    links = [copies(level, *bufs[level]) for level in range(3)]
    for clear, _, _, _ in links:
        clear()

    def put_row(level, row, value):
        _, hp, side_out, _, _ = bufs[level]
        length = value.shape[0]
        hp[row + 1] = value
        side_out[0, pl.ds(row, 1), :] = value[0:8, :].astype(F32)[0:1, :]
        side_out[1, pl.ds(row, 1), :] = value[length - 16 :, :].astype(F32)[15:16, :]

    def send_all(level):
        count, _, side_out, _, corner_out = bufs[level]
        depth = side_out.shape[2]
        for end, row in ((0, 0), (1, count - 1)):
            for side in range(2):
                corner_out[2 * end + side] = jnp.broadcast_to(
                    side_out[side, row : row + 1, :], (8, depth)
                )
        links[level][1]((2, 3, 0, 1, 4, 5, 6, 7))

    def receive_all(level):
        links[level][2](range(8))

    def tap_sum(parts):
        length, depth = parts.shape[0], parts.shape[1] // 3
        at = lax.broadcasted_iota(jnp.int32, (8, depth), 0)
        before = pltpu.roll(parts[:, 0:depth], 1, axis=0)
        after = pltpu.roll(parts[:, 2 * depth :], length - 1, axis=0)
        before = jnp.concatenate([jnp.where(at == 0, 0.0, before[0:8]), before[8:]], axis=0)
        after = jnp.concatenate(
            [after[: length - 8], jnp.where(at == 7, 0.0, after[length - 8 :])], axis=0
        )
        return before + parts[:, depth : 2 * depth] + after

    def side_terms(level, term, left, right):
        count, _, _, side_in, _ = bufs[level]
        for side, weights in ((0, left), (1, right)):
            lhs = jnp.concatenate(
                [side_in[side, 7 + tap : 7 + tap + count, :] for tap in range(3)], axis=1
            )
            term[side] = dot(lhs.astype(BF16), weights)

    def summed(acc, term, row):
        length, depth = acc.shape[1], acc.shape[2]
        at = lax.broadcasted_iota(jnp.int32, (8, depth), 0)
        head = acc[row, 0:8, :] + jnp.where(at == 0, term[0, pl.ds(row, 1), :], 0.0)
        tail = acc[row, length - 8 : length, :] + jnp.where(
            at == 7, term[1, pl.ds(row, 1), :], 0.0
        )
        return jnp.concatenate([head, acc[row, 8 : length - 8, :], tail], axis=0)

    level_now = jnp.full((1, c1), now_ref[0], F32)
    scale_in = 1.0 / jnp.sqrt(level_now * level_now + 1.0)
    scale_one = scale_in[0:1, 0:1]
    load_small[0].wait()
    noisy_t[...] = jnp.transpose(scale_one * noisy_ref[...])
    mine = noisy_t[pl.ds(first, cols), :]
    load_small[1].wait()
    proj = proj_ref[...]
    load_cond.wait()
    for row in range(height):
        value = cond[row].astype(F32) + mine[:, row : row + 1] * proj
        put_row(0, row, value.astype(BF16))
    pl.semaphore_wait(barrier, greeted)
    send_all(0)

    def fine_pairs(layer, hp, group):
        lhs = jnp.concatenate(
            [jnp.concatenate([hp[2 * i + j] for j in range(4)], axis=1) for i in group], axis=0
        )
        parts = dot(lhs, wf[layer].reshape(4 * c1, 6 * c1))
        for k, i in enumerate(group):
            for j in range(2):
                acc0[2 * i + j] = tap_sum(
                    parts[k * cols : (k + 1) * cols, 3 * j * c1 : 3 * (j + 1) * c1]
                )

    def fine_conv(layer, level, hp):
        for copy in load_fine[layer]:
            copy.wait()

        def body(step, carry):
            fine_pairs(layer, hp, (1 + 2 * step, 2 + 2 * step))
            return carry

        lax.fori_loop(0, pairs // 2 - 1, body, 0)
        receive_all(level)
        fine_pairs(layer, hp, (0, pairs - 1))
        side_terms(
            level, term0,
            wf[layer, 0:3, :, 0:c1].reshape(3 * c1, c1),
            wf[layer, 0:3, :, 2 * c1 : 3 * c1].reshape(3 * c1, c1),
        )

    pool_at = lax.broadcasted_iota(jnp.int32, (half, 2 * cols), 1)
    pool_to = lax.broadcasted_iota(jnp.int32, (half, 2 * cols), 0)
    pool_at = jnp.where(pool_at >= cols, pool_at - cols, pool_at)
    pool = jnp.where(jnp.right_shift(pool_at, 1) == pool_to, 0.25, 0.0).astype(BF16)

    def first_end(step, carry):
        pooled = []
        for k in range(2):
            both = []
            for j in range(2):
                row = 4 * step + 2 * k + j
                value = hp0[row + 1].astype(F32) + silu(summed(acc0, term0, row))
                value = value.astype(BF16)
                h1[row] = value
                both.append(value)
            pooled.append(dot(pool, jnp.concatenate(both, axis=0)).astype(BF16))
        lower = dot(jnp.concatenate(pooled, axis=0), down_ref[...]).astype(BF16)
        for k in range(2):
            put_row(1, 2 * step + k, lower[k * half : (k + 1) * half])
        return carry

    fine_conv(0, 0, hp0)
    load_small[2].wait()
    lax.fori_loop(0, pairs // 2, first_end, 0)
    send_all(1)

    lift_at = lax.broadcasted_iota(jnp.int32, (cols, half), 0)
    lift_to = lax.broadcasted_iota(jnp.int32, (cols, half), 1)
    lift = jnp.where(jnp.right_shift(lift_at, 1) == lift_to, 1.0, 0.0).astype(BF16)

    def coarse_rows(group):
        lhs = jnp.concatenate(
            [jnp.concatenate([hp1[i + j] for j in range(3)], axis=1) for i in group], axis=0
        )
        parts = dot(lhs, wc[...].reshape(3 * c2, 3 * c2))
        for k, i in enumerate(group):
            acc1[i] = tap_sum(parts[k * half : (k + 1) * half])

    def second_start(step, carry):
        wide = []
        for k in range(2):
            i = 2 * step + k
            value = hp1[i + 1].astype(F32) + silu(summed(acc1, term1, i))
            wide.append(dot(lift, value.astype(BF16)).astype(BF16))
        lifted = dot(jnp.concatenate(wide, axis=0), up_ref[...])
        for k in range(2):
            for j in range(2):
                row = 4 * step + 2 * k + j
                value = h1[row].astype(F32) + lifted[k * cols : (k + 1) * cols]
                put_row(2, row, value.astype(BF16))
        return carry

    for copy in load_coarse:
        copy.wait()
    load_small[3].wait()
    coarse_rows(range(1, pairs - 1))
    receive_all(1)
    coarse_rows((0, pairs - 1))
    side_terms(
        1, term1,
        wc[:, :, 0:c2].reshape(3 * c2, c2),
        wc[:, :, 2 * c2 : 3 * c2].reshape(3 * c2, c2),
    )
    lax.fori_loop(0, pairs // 2, second_start, 0)
    send_all(2)

    load_small[4].wait()
    outp = jnp.broadcast_to(outp_ref[...].astype(F32), (16, c1)).astype(BF16)

    def second_end(step, carry):
        for k in range(4):
            row = 4 * step + k
            value = hp2[row + 1].astype(F32) + silu(summed(acc0, term0, row))
            total = lax.dot_general(
                outp, value.astype(BF16), (((1,), (1,)), ((), ())), preferred_element_type=F32
            )
            net[g, pl.ds(row, 1), :] = total[0:1, :]
        return carry

    fine_conv(1, 2, hp2)
    lax.fori_loop(0, height // 4, second_end, 0)

    shares = []
    for step in range(1, n_rep):
        share = pltpu.make_async_remote_copy(
            src_ref=net.at[g],
            dst_ref=net.at[g],
            send_sem=net_send.at[step - 1],
            recv_sem=net_recv.at[step - 1],
            device_id={"fsdp": lax.rem(f + step, n_rep)},
            device_id_type=MESH,
        )
        share.start()
        shares.append(share)
    for _, _, _, finish in links:
        finish()
    for step in range(1, n_rep):
        owner = place(lax.rem(f + n_rep - step, n_rep), s)
        pltpu.make_async_remote_copy(
            src_ref=net.at[owner],
            dst_ref=net.at[owner],
            send_sem=net_send.at[step - 1],
            recv_sem=net_recv.at[step - 1],
            device_id={"fsdp": lax.rem(f + step, n_rep)},
            device_id_type=MESH,
        ).wait_recv()
    for share in shares:
        share.wait_send()

    load_small[5].wait()

    network = jnp.concatenate([net[k] for k in range(n_rep)], axis=1)
    level_next = jnp.full((1, c1), next_ref[0], F32)
    scale_skip = (1.0 / (level_now * level_now + 1.0))[0:1, 0:1]
    scale_out = (level_now * scale_in)[0:1, 0:1]
    ratio = (level_next / level_now)[0:1, 0:1]
    spread = jnp.sqrt(level_now * level_now - level_next * level_next)[0:1, 0:1]
    noisy = noisy_ref[...]
    denoised = scale_skip * noisy + scale_out * network
    out_ref[...] = denoised + ratio * (noisy - denoised) + spread * draw_ref[...]


def per_device(
    sizes,
    noisy_field, noise_draw, cond_features, sigma_now, sigma_next, field_proj,
    fine_kernels, coarse_kernel, down_proj, up_proj, out_proj,
):
    n_rep = sizes[1]
    height, breadth, c1 = cond_features.shape
    c2 = coarse_kernel.shape[2]
    cols = breadth // n_rep
    pairs, half = height // 2, cols // 2

    def level_bufs(rows, depth):
        return [
            pltpu.VMEM((2, rows, depth), F32),
            pltpu.VMEM((2, rows + 16, depth), F32),
            pltpu.VMEM((4, 8, depth), F32),
        ]

    smem = pl.BlockSpec(memory_space=pltpu.SMEM)
    vmem = pl.BlockSpec(memory_space=pltpu.VMEM)
    hbm = pl.BlockSpec(memory_space=pltpu.HBM)
    return pl.pallas_call(
        functools.partial(kernel, sizes),
        out_shape=jax.ShapeDtypeStruct((height, breadth), F32),
        in_specs=[smem] * 2 + [hbm] * 9,
        out_specs=vmem,
        scratch_shapes=[
            pltpu.VMEM((height, breadth), F32),
            pltpu.VMEM((height, breadth), F32),
            pltpu.VMEM((1, c1), F32),
            pltpu.VMEM((1, c1), BF16),
            pltpu.VMEM((c1, c2), BF16),
            pltpu.VMEM((c2, c1), BF16),
            pltpu.VMEM((height, cols, c1), BF16),
            pltpu.VMEM((2, 4, c1, 6 * c1), BF16),
            pltpu.VMEM((3, c2, 3 * c2), BF16),
            pltpu.VMEM((height + 2, cols, c1), BF16),
            pltpu.VMEM((pairs + 2, half, c2), BF16),
            pltpu.VMEM((height + 2, cols, c1), BF16),
            pltpu.VMEM((height, cols, c1), BF16),
            pltpu.VMEM((breadth, height), F32),
            pltpu.VMEM((height, cols, c1), F32),
            pltpu.VMEM((pairs, half, c2), F32),
            pltpu.VMEM((2, height, c1), F32),
            pltpu.VMEM((2, pairs, c2), F32),
            pltpu.VMEM((n_rep, height, cols), F32),
        ]
        + level_bufs(height, c1)
        + level_bufs(pairs, c2)
        + level_bufs(height, c1)
        + [
            pltpu.SemaphoreType.DMA((22,)),
            pltpu.SemaphoreType.DMA((3, 8)),
            pltpu.SemaphoreType.DMA((3, 8)),
            pltpu.SemaphoreType.DMA((max(n_rep - 1, 1),)),
            pltpu.SemaphoreType.DMA((max(n_rep - 1, 1),)),
        ],
        compiler_params=pltpu.CompilerParams(
            collective_id=0, has_side_effects=True, vmem_limit_bytes=63 * 1024 * 1024
        ),
    )(
        sigma_now, sigma_next, noisy_field, noise_draw,
        field_proj.reshape(1, c1), out_proj.reshape(1, c1), down_proj, up_proj,
        cond_features,
        fine_kernels.reshape(2, 3, 3, c1, c1), coarse_kernel.reshape(3, 3, c2, c2),
    )


def solution(mesh):
    sizes = (mesh.shape["patch"], mesh.shape["fsdp"], mesh.shape["sub"])
    field = P(("groups", "patch"), "sub")
    return jax.shard_map(
        functools.partial(per_device, sizes),
        mesh=mesh,
        in_specs=(field, field, P(("groups", "patch"), "sub", None)) + (P(),) * 8,
        out_specs=field,
        check_vma=False,
    )
```

```python
import functools
import jax
import jax.numpy as jnp
from jax import lax
from jax.experimental import pallas as pl
from jax.experimental.pallas import tpu as pltpu
from jax.sharding import PartitionSpec as P

MESH = pl.DeviceIdType.MESH
BF16 = jnp.bfloat16
F32 = jnp.float32

WAYS = ((-1, 0), (1, 0), (0, -1), (0, 1), (-1, -1), (-1, 1), (1, -1), (1, 1))
BACK = (1, 0, 3, 2, 7, 6, 5, 4)


def silu(v):
    return (0.5 * v) * (1.0 + jnp.tanh(0.5 * v))


def dot(a, b):
    return jnp.dot(a, b, preferred_element_type=F32)


def kernel(
    sizes,
    now_ref, next_ref, noisy_hbm, draw_hbm, proj_hbm, outp_hbm, down_hbm, up_hbm,
    cond_hbm, fine_hbm, coarse_hbm,
    out_ref,
    noisy_ref, draw_ref, proj_ref, outp_ref, down_ref, up_ref,
    cond, wf, wc, hp0, hp1, hp2, h1, noisy_t, acc0, acc1, term0, term1, net,
    side_out0, side_in0, corner_out0,
    side_out1, side_in1, corner_out1,
    side_out2, side_in2, corner_out2,
    load_sem, send_sem, recv_sem, net_send, net_recv,
):
    n_patch, n_rep, n_sub = sizes
    n_part = n_rep * n_sub
    height, cols, c1 = cond.shape
    pairs = height // 2
    half = cols // 2
    c2 = wc.shape[1]

    p = lax.axis_index("patch")
    f = lax.axis_index("fsdp")
    s = lax.axis_index("sub")

    def place(rep, sub):
        return rep + lax.rem(sub, 2) * (n_rep - 1 - 2 * rep)

    g = place(f, s)
    q = s * n_rep + g

    across = []
    for other in (q - 1, q, q + 1):
        other_s = lax.div(other, n_rep)
        across.append((place(other - other_s * n_rep, other_s), other_s))
    inside_p = {-1: p > 0, 1: p < n_patch - 1}
    inside_q = {-1: q > 0, 1: q < n_part - 1}
    devices, inside = [], []
    for dp, dq in WAYS:
        to_f, to_s = across[dq + 1]
        devices.append({"patch": p + dp, "fsdp": to_f, "sub": to_s})
        if dp == 0:
            inside.append(inside_q[dq])
        elif dq == 0:
            inside.append(inside_p[dp])
        else:
            inside.append(jnp.logical_and(inside_p[dp], inside_q[dq]))

    def device(way):
        return devices[way]

    def has(way):
        return inside[way]

    barrier = pltpu.get_barrier_semaphore()
    greeted = n_rep - 1
    for way in range(8):
        there = has(way)

        @pl.when(there)
        def _(way=way):
            pl.semaphore_signal(barrier, inc=1, device_id=device(way), device_id_type=MESH)

        greeted = greeted + there.astype(jnp.int32)
    for step in range(1, n_rep):
        pl.semaphore_signal(
            barrier, inc=1, device_id={"fsdp": lax.rem(f + step, n_rep)}, device_id_type=MESH
        )

    first = pl.multiple_of(g * cols, cols)
    load_cond = pltpu.make_async_copy(cond_hbm.at[:, pl.ds(first, cols), :], cond, load_sem.at[21])
    load_small = [
        pltpu.make_async_copy(src, dst, load_sem.at[k])
        for k, (src, dst) in enumerate(
            (
                (noisy_hbm, noisy_ref),
                (proj_hbm, proj_ref),
                (down_hbm, down_ref),
                (up_hbm, up_ref),
                (outp_hbm, outp_ref),
                (draw_hbm, draw_ref),
            )
        )
    ]
    load_small[0].start()
    load_small[1].start()
    load_cond.start()
    wf[:, 3:4, :, 0 : 3 * c1] = jnp.zeros((2, 1, c1, 3 * c1), BF16)
    wf[:, 0:1, :, 3 * c1 :] = jnp.zeros((2, 1, c1, 3 * c1), BF16)
    load_fine = [
        [
            pltpu.make_async_copy(
                fine_hbm.at[layer, :, tap],
                wf.at[layer, low : low + 3, :, (3 * low + tap) * c1 : (3 * low + tap + 1) * c1],
                load_sem.at[6 + 6 * layer + 3 * low + tap],
            )
            for low in range(2)
            for tap in range(3)
        ]
        for layer in range(2)
    ]
    load_coarse = [
        pltpu.make_async_copy(
            coarse_hbm.at[:, tap], wc.at[:, :, tap * c2 : (tap + 1) * c2], load_sem.at[18 + tap]
        )
        for tap in range(3)
    ]
    for copy in load_fine[0] + [load_small[2]] + load_coarse + [load_small[3]] + load_fine[1]:
        copy.start()
    load_small[4].start()
    load_small[5].start()

    def copies(level, count, hp, side_out, side_in, corner_out):
        own = pl.ds(8, count)
        above = pl.ds(0, 8)
        below = pl.ds(count + 8, 8)
        routes = [
            (hp.at[1], hp.at[count + 1]),
            (hp.at[count], hp.at[0]),
            (side_out.at[0], side_in.at[1, own, :]),
            (side_out.at[1], side_in.at[0, own, :]),
            (corner_out.at[0], side_in.at[1, below, :]),
            (corner_out.at[1], side_in.at[0, below, :]),
            (corner_out.at[2], side_in.at[1, above, :]),
            (corner_out.at[3], side_in.at[0, above, :]),
        ]

        def copy(way):
            return pltpu.make_async_remote_copy(
                src_ref=routes[way][0],
                dst_ref=routes[way][1],
                send_sem=send_sem.at[level, way],
                recv_sem=recv_sem.at[level, way],
                device_id=device(way),
                device_id_type=MESH,
            )

        def clear():
            for way in range(8):
                @pl.when(jnp.logical_not(has(BACK[way])))
                def _(way=way):
                    into = routes[way][1]
                    into[...] = jnp.zeros(into.shape, into.dtype)

        def send(ways):
            for way in ways:
                @pl.when(has(way))
                def _(way=way):
                    copy(way).start()

        def receive(ways):
            for way in ways:
                @pl.when(has(BACK[way]))
                def _(way=way):
                    copy(way).wait_recv()

        def finish():
            for way in range(8):
                @pl.when(has(way))
                def _(way=way):
                    copy(way).wait_send()

        return clear, send, receive, finish

    bufs = (
        (height, hp0, side_out0, side_in0, corner_out0),
        (pairs, hp1, side_out1, side_in1, corner_out1),
        (height, hp2, side_out2, side_in2, corner_out2),
    )
    links = [copies(level, *bufs[level]) for level in range(3)]
    for clear, _, _, _ in links:
        clear()

    def put_row(level, row, value):
        _, hp, side_out, _, _ = bufs[level]
        length = value.shape[0]
        hp[row + 1] = value
        side_out[0, pl.ds(row, 1), :] = value[0:8, :].astype(F32)[0:1, :]
        side_out[1, pl.ds(row, 1), :] = value[length - 16 :, :].astype(F32)[15:16, :]

    def send_rows(level):
        count, _, side_out, _, corner_out = bufs[level]
        depth = side_out.shape[2]
        for end, row in ((0, 0), (1, count - 1)):
            for side in range(2):
                corner_out[2 * end + side] = jnp.broadcast_to(
                    side_out[side, row : row + 1, :], (8, depth)
                )
        links[level][1]((0, 1, 4, 5, 6, 7))

    def send_sides(level):
        links[level][1]((2, 3))

    def receive_sides(level):
        links[level][2]((2, 3, 4, 5, 6, 7))

    def receive_rows(level):
        links[level][2]((0, 1))

    def tap_sum(parts):
        length, depth = parts.shape[0], parts.shape[1] // 3
        at = lax.broadcasted_iota(jnp.int32, (8, depth), 0)
        before = pltpu.roll(parts[:, 0:depth], 1, axis=0)
        after = pltpu.roll(parts[:, 2 * depth :], length - 1, axis=0)
        before = jnp.concatenate([jnp.where(at == 0, 0.0, before[0:8]), before[8:]], axis=0)
        after = jnp.concatenate(
            [after[: length - 8], jnp.where(at == 7, 0.0, after[length - 8 :])], axis=0
        )
        return before + parts[:, depth : 2 * depth] + after

    def side_terms(level, term, left, right):
        count, _, _, side_in, _ = bufs[level]
        for side, weights in ((0, left), (1, right)):
            lhs = jnp.concatenate(
                [side_in[side, 7 + tap : 7 + tap + count, :] for tap in range(3)], axis=1
            )
            term[side] = dot(lhs.astype(BF16), weights)

    def summed(acc, term, row):
        length, depth = acc.shape[1], acc.shape[2]
        at = lax.broadcasted_iota(jnp.int32, (8, depth), 0)
        head = acc[row, 0:8, :] + jnp.where(at == 0, term[0, pl.ds(row, 1), :], 0.0)
        tail = acc[row, length - 8 : length, :] + jnp.where(
            at == 7, term[1, pl.ds(row, 1), :], 0.0
        )
        return jnp.concatenate([head, acc[row, 8 : length - 8, :], tail], axis=0)

    level_now = jnp.full((1, c1), now_ref[0], F32)
    scale_in = 1.0 / jnp.sqrt(level_now * level_now + 1.0)
    scale_one = scale_in[0:1, 0:1]
    load_small[0].wait()
    noisy_t[...] = jnp.transpose(scale_one * noisy_ref[...])
    mine = noisy_t[pl.ds(first, cols), :]
    load_small[1].wait()
    proj = proj_ref[...]
    load_cond.wait()
    for row in range(height):
        value = cond[row].astype(F32) + mine[:, row : row + 1] * proj
        put_row(0, row, value.astype(BF16))
    pl.semaphore_wait(barrier, greeted)
    send_rows(0)
    send_sides(0)

    def fine_pairs(layer, hp, group):
        lhs = jnp.concatenate(
            [jnp.concatenate([hp[2 * i + j] for j in range(4)], axis=1) for i in group], axis=0
        )
        parts = dot(lhs, wf[layer].reshape(4 * c1, 6 * c1))
        for k, i in enumerate(group):
            for j in range(2):
                acc0[2 * i + j] = tap_sum(
                    parts[k * cols : (k + 1) * cols, 3 * j * c1 : 3 * (j + 1) * c1]
                )

    border = (0, pairs - 1)

    def over_inner(work):
        def body(step, carry):
            work((1 + 2 * step, 2 + 2 * step))
            return carry

        lax.fori_loop(0, pairs // 2 - 1, body, 0)

    def fine_inner(layer, hp):
        for copy in load_fine[layer]:
            copy.wait()
        over_inner(lambda group: fine_pairs(layer, hp, group))

    def fine_sides(layer, level):
        receive_sides(level)
        side_terms(
            level, term0,
            wf[layer, 0:3, :, 0:c1].reshape(3 * c1, c1),
            wf[layer, 0:3, :, 2 * c1 : 3 * c1].reshape(3 * c1, c1),
        )

    pool_at = lax.broadcasted_iota(jnp.int32, (half, 2 * cols), 1)
    pool_to = lax.broadcasted_iota(jnp.int32, (half, 2 * cols), 0)
    pool_at = jnp.where(pool_at >= cols, pool_at - cols, pool_at)
    pool = jnp.where(jnp.right_shift(pool_at, 1) == pool_to, 0.25, 0.0).astype(BF16)

    def first_end(group):
        pooled = []
        for i in group:
            both = []
            for j in range(2):
                row = 2 * i + j
                value = hp0[row + 1].astype(F32) + silu(summed(acc0, term0, row))
                value = value.astype(BF16)
                h1[row] = value
                both.append(value)
            pooled.append(dot(pool, jnp.concatenate(both, axis=0)).astype(BF16))
        lower = dot(jnp.concatenate(pooled, axis=0), down_ref[...]).astype(BF16)
        for k, i in enumerate(group):
            put_row(1, i, lower[k * half : (k + 1) * half])

    fine_inner(0, hp0)
    load_small[2].wait()
    fine_sides(0, 0)
    receive_rows(0)
    fine_pairs(0, hp0, border)
    first_end(border)
    send_rows(1)
    over_inner(first_end)
    send_sides(1)

    lift_at = lax.broadcasted_iota(jnp.int32, (cols, half), 0)
    lift_to = lax.broadcasted_iota(jnp.int32, (cols, half), 1)
    lift = jnp.where(jnp.right_shift(lift_at, 1) == lift_to, 1.0, 0.0).astype(BF16)

    def coarse_rows(group):
        lhs = jnp.concatenate(
            [jnp.concatenate([hp1[i + j] for j in range(3)], axis=1) for i in group], axis=0
        )
        parts = dot(lhs, wc[...].reshape(3 * c2, 3 * c2))
        for k, i in enumerate(group):
            acc1[i] = tap_sum(parts[k * half : (k + 1) * half])

    def second_start(group):
        wide = []
        for i in group:
            value = hp1[i + 1].astype(F32) + silu(summed(acc1, term1, i))
            wide.append(dot(lift, value.astype(BF16)).astype(BF16))
        lifted = dot(jnp.concatenate(wide, axis=0), up_ref[...])
        for k, i in enumerate(group):
            for j in range(2):
                row = 2 * i + j
                value = h1[row].astype(F32) + lifted[k * cols : (k + 1) * cols]
                put_row(2, row, value.astype(BF16))

    for copy in load_coarse:
        copy.wait()
    load_small[3].wait()
    coarse_rows(range(1, pairs - 1))
    receive_sides(1)
    side_terms(
        1, term1,
        wc[:, :, 0:c2].reshape(3 * c2, c2),
        wc[:, :, 2 * c2 : 3 * c2].reshape(3 * c2, c2),
    )
    receive_rows(1)
    coarse_rows(border)
    second_start(border)
    send_rows(2)
    over_inner(second_start)
    send_sides(2)

    load_small[4].wait()
    outp = jnp.broadcast_to(outp_ref[...].astype(F32), (16, c1)).astype(BF16)

    def second_end(group):
        for i in group:
            for j in range(2):
                row = 2 * i + j
                value = hp2[row + 1].astype(F32) + silu(summed(acc0, term0, row))
                total = lax.dot_general(
                    outp, value.astype(BF16), (((1,), (1,)), ((), ())),
                    preferred_element_type=F32,
                )
                net[g, pl.ds(row, 1), :] = total[0:1, :]

    fine_inner(1, hp2)
    fine_sides(1, 2)
    over_inner(second_end)
    receive_rows(2)
    fine_pairs(1, hp2, border)
    second_end(border)

    shares = []
    for step in range(1, n_rep):
        share = pltpu.make_async_remote_copy(
            src_ref=net.at[g],
            dst_ref=net.at[g],
            send_sem=net_send.at[step - 1],
            recv_sem=net_recv.at[step - 1],
            device_id={"fsdp": lax.rem(f + step, n_rep)},
            device_id_type=MESH,
        )
        share.start()
        shares.append(share)
    for _, _, _, finish in links:
        finish()
    for step in range(1, n_rep):
        owner = place(lax.rem(f + n_rep - step, n_rep), s)
        pltpu.make_async_remote_copy(
            src_ref=net.at[owner],
            dst_ref=net.at[owner],
            send_sem=net_send.at[step - 1],
            recv_sem=net_recv.at[step - 1],
            device_id={"fsdp": lax.rem(f + step, n_rep)},
            device_id_type=MESH,
        ).wait_recv()
    for share in shares:
        share.wait_send()

    load_small[5].wait()

    network = jnp.concatenate([net[k] for k in range(n_rep)], axis=1)
    level_next = jnp.full((1, c1), next_ref[0], F32)
    scale_skip = (1.0 / (level_now * level_now + 1.0))[0:1, 0:1]
    scale_out = (level_now * scale_in)[0:1, 0:1]
    ratio = (level_next / level_now)[0:1, 0:1]
    spread = jnp.sqrt(level_now * level_now - level_next * level_next)[0:1, 0:1]
    noisy = noisy_ref[...]
    denoised = scale_skip * noisy + scale_out * network
    out_ref[...] = denoised + ratio * (noisy - denoised) + spread * draw_ref[...]


def per_device(
    sizes,
    noisy_field, noise_draw, cond_features, sigma_now, sigma_next, field_proj,
    fine_kernels, coarse_kernel, down_proj, up_proj, out_proj,
):
    n_rep = sizes[1]
    height, breadth, c1 = cond_features.shape
    c2 = coarse_kernel.shape[2]
    cols = breadth // n_rep
    pairs, half = height // 2, cols // 2

    def level_bufs(rows, depth):
        return [
            pltpu.VMEM((2, rows, depth), F32),
            pltpu.VMEM((2, rows + 16, depth), F32),
            pltpu.VMEM((4, 8, depth), F32),
        ]

    smem = pl.BlockSpec(memory_space=pltpu.SMEM)
    vmem = pl.BlockSpec(memory_space=pltpu.VMEM)
    hbm = pl.BlockSpec(memory_space=pltpu.HBM)
    return pl.pallas_call(
        functools.partial(kernel, sizes),
        out_shape=jax.ShapeDtypeStruct((height, breadth), F32),
        in_specs=[smem] * 2 + [hbm] * 9,
        out_specs=vmem,
        scratch_shapes=[
            pltpu.VMEM((height, breadth), F32),
            pltpu.VMEM((height, breadth), F32),
            pltpu.VMEM((1, c1), F32),
            pltpu.VMEM((1, c1), BF16),
            pltpu.VMEM((c1, c2), BF16),
            pltpu.VMEM((c2, c1), BF16),
            pltpu.VMEM((height, cols, c1), BF16),
            pltpu.VMEM((2, 4, c1, 6 * c1), BF16),
            pltpu.VMEM((3, c2, 3 * c2), BF16),
            pltpu.VMEM((height + 2, cols, c1), BF16),
            pltpu.VMEM((pairs + 2, half, c2), BF16),
            pltpu.VMEM((height + 2, cols, c1), BF16),
            pltpu.VMEM((height, cols, c1), BF16),
            pltpu.VMEM((breadth, height), F32),
            pltpu.VMEM((height, cols, c1), F32),
            pltpu.VMEM((pairs, half, c2), F32),
            pltpu.VMEM((2, height, c1), F32),
            pltpu.VMEM((2, pairs, c2), F32),
            pltpu.VMEM((n_rep, height, cols), F32),
        ]
        + level_bufs(height, c1)
        + level_bufs(pairs, c2)
        + level_bufs(height, c1)
        + [
            pltpu.SemaphoreType.DMA((22,)),
            pltpu.SemaphoreType.DMA((3, 8)),
            pltpu.SemaphoreType.DMA((3, 8)),
            pltpu.SemaphoreType.DMA((max(n_rep - 1, 1),)),
            pltpu.SemaphoreType.DMA((max(n_rep - 1, 1),)),
        ],
        compiler_params=pltpu.CompilerParams(
            collective_id=0, has_side_effects=True, vmem_limit_bytes=63 * 1024 * 1024
        ),
    )(
        sigma_now, sigma_next, noisy_field, noise_draw,
        field_proj.reshape(1, c1), out_proj.reshape(1, c1), down_proj, up_proj,
        cond_features,
        fine_kernels.reshape(2, 3, 3, c1, c1), coarse_kernel.reshape(3, 3, c2, c2),
    )


def solution(mesh):
    sizes = (mesh.shape["patch"], mesh.shape["fsdp"], mesh.shape["sub"])
    field = P(("groups", "patch"), "sub")
    return jax.shard_map(
        functools.partial(per_device, sizes),
        mesh=mesh,
        in_specs=(field, field, P(("groups", "patch"), "sub", None)) + (P(),) * 8,
        out_specs=field,
        check_vma=False,
    )
```

```python
import functools
import jax
import jax.numpy as jnp
from jax import lax
from jax.experimental import pallas as pl
from jax.experimental.pallas import tpu as pltpu
from jax.sharding import PartitionSpec as P

MESH = pl.DeviceIdType.MESH
BF16 = jnp.bfloat16
F32 = jnp.float32

WAYS = ((-1, 0), (1, 0), (0, -1), (0, 1), (-1, -1), (-1, 1), (1, -1), (1, 1))
BACK = (1, 0, 3, 2, 7, 6, 5, 4)


def silu(v):
    return (0.5 * v) * (1.0 + jnp.tanh(0.5 * v))


def dot(a, b):
    return jnp.dot(a, b, preferred_element_type=F32)


def kernel(
    sizes,
    now_ref, next_ref, noisy_hbm, draw_hbm, proj_hbm, outp_hbm, down_hbm, up_hbm,
    cond_hbm, fine_hbm, coarse_hbm,
    out_ref,
    noisy_ref, draw_ref, proj_ref, outp_ref, down_ref, up_ref,
    cond, wf, wc, hp0, hp1, hp2, h1, noisy_t, acc0, acc1, term0, term1, net,
    side_out0, side_in0, corner_out0,
    side_out1, side_in1, corner_out1,
    side_out2, side_in2, corner_out2,
    load_sem, send_sem, recv_sem, net_send, net_recv,
):
    n_patch, n_rep, n_sub = sizes
    n_part = n_rep * n_sub
    height, cols, c1 = cond.shape
    pairs = height // 2
    half = cols // 2
    c2 = wc.shape[1]

    p = lax.axis_index("patch")
    f = lax.axis_index("fsdp")
    s = lax.axis_index("sub")

    def place(rep, sub):
        return rep + lax.rem(sub, 2) * (n_rep - 1 - 2 * rep)

    g = place(f, s)
    q = s * n_rep + g

    across = []
    for other in (q - 1, q, q + 1):
        other_s = lax.div(other, n_rep)
        across.append((place(other - other_s * n_rep, other_s), other_s))
    inside_p = {-1: p > 0, 1: p < n_patch - 1}
    inside_q = {-1: q > 0, 1: q < n_part - 1}
    devices, inside = [], []
    for dp, dq in WAYS:
        to_f, to_s = across[dq + 1]
        devices.append({"patch": p + dp, "fsdp": to_f, "sub": to_s})
        if dp == 0:
            inside.append(inside_q[dq])
        elif dq == 0:
            inside.append(inside_p[dp])
        else:
            inside.append(jnp.logical_and(inside_p[dp], inside_q[dq]))

    def device(way):
        return devices[way]

    def has(way):
        return inside[way]

    barrier = pltpu.get_barrier_semaphore()
    greeted = n_rep - 1
    for way in range(8):
        there = has(way)

        @pl.when(there)
        def _(way=way):
            pl.semaphore_signal(barrier, inc=1, device_id=device(way), device_id_type=MESH)

        greeted = greeted + there.astype(jnp.int32)
    for step in range(1, n_rep):
        pl.semaphore_signal(
            barrier, inc=1, device_id={"fsdp": lax.rem(f + step, n_rep)}, device_id_type=MESH
        )

    first = pl.multiple_of(g * cols, cols)
    load_cond = pltpu.make_async_copy(cond_hbm.at[:, pl.ds(first, cols), :], cond, load_sem.at[21])
    load_small = [
        pltpu.make_async_copy(src, dst, load_sem.at[k])
        for k, (src, dst) in enumerate(
            (
                (noisy_hbm, noisy_ref),
                (proj_hbm, proj_ref),
                (down_hbm, down_ref),
                (up_hbm, up_ref),
                (outp_hbm, outp_ref),
                (draw_hbm, draw_ref),
            )
        )
    ]
    load_small[0].start()
    load_small[1].start()
    load_cond.start()
    wf[:, 3:4, :, 0 : 3 * c1] = jnp.zeros((2, 1, c1, 3 * c1), BF16)
    wf[:, 0:1, :, 3 * c1 :] = jnp.zeros((2, 1, c1, 3 * c1), BF16)
    load_fine = [
        [
            pltpu.make_async_copy(
                fine_hbm.at[layer, :, tap],
                wf.at[layer, low : low + 3, :, (3 * low + tap) * c1 : (3 * low + tap + 1) * c1],
                load_sem.at[6 + 6 * layer + 3 * low + tap],
            )
            for low in range(2)
            for tap in range(3)
        ]
        for layer in range(2)
    ]
    load_coarse = [
        pltpu.make_async_copy(
            coarse_hbm.at[:, tap], wc.at[:, :, tap * c2 : (tap + 1) * c2], load_sem.at[18 + tap]
        )
        for tap in range(3)
    ]
    for copy in load_fine[0] + [load_small[2]] + load_coarse + [load_small[3]] + load_fine[1]:
        copy.start()
    load_small[4].start()
    load_small[5].start()

    def copies(level, count, hp, side_out, side_in, corner_out):
        own = pl.ds(8, count)
        above = pl.ds(0, 8)
        below = pl.ds(count + 8, 8)
        routes = [
            (hp.at[1], hp.at[count + 1]),
            (hp.at[count], hp.at[0]),
            (side_out.at[0], side_in.at[1, own, :]),
            (side_out.at[1], side_in.at[0, own, :]),
            (corner_out.at[0], side_in.at[1, below, :]),
            (corner_out.at[1], side_in.at[0, below, :]),
            (corner_out.at[2], side_in.at[1, above, :]),
            (corner_out.at[3], side_in.at[0, above, :]),
        ]

        def copy(way):
            return pltpu.make_async_remote_copy(
                src_ref=routes[way][0],
                dst_ref=routes[way][1],
                send_sem=send_sem.at[level, way],
                recv_sem=recv_sem.at[level, way],
                device_id=device(way),
                device_id_type=MESH,
            )

        def clear():
            for way in range(8):
                @pl.when(jnp.logical_not(has(BACK[way])))
                def _(way=way):
                    into = routes[way][1]
                    into[...] = jnp.zeros(into.shape, into.dtype)

        def send(ways):
            for way in ways:
                @pl.when(has(way))
                def _(way=way):
                    copy(way).start()

        def receive(ways):
            for way in ways:
                @pl.when(has(BACK[way]))
                def _(way=way):
                    copy(way).wait_recv()

        def finish():
            for way in range(8):
                @pl.when(has(way))
                def _(way=way):
                    copy(way).wait_send()

        return clear, send, receive, finish

    bufs = (
        (height, hp0, side_out0, side_in0, corner_out0),
        (pairs, hp1, side_out1, side_in1, corner_out1),
        (height, hp2, side_out2, side_in2, corner_out2),
    )
    links = [copies(level, *bufs[level]) for level in range(3)]
    for clear, _, _, _ in links:
        clear()

    def put_row(level, row, value):
        _, hp, side_out, _, _ = bufs[level]
        length = value.shape[0]
        hp[row + 1] = value
        side_out[0, pl.ds(row, 1), :] = value[0:8, :].astype(F32)[0:1, :]
        side_out[1, pl.ds(row, 1), :] = value[length - 16 :, :].astype(F32)[15:16, :]

    def send_rows(level):
        count, _, side_out, _, corner_out = bufs[level]
        depth = side_out.shape[2]
        for end, row in ((0, 0), (1, count - 1)):
            for side in range(2):
                corner_out[2 * end + side] = jnp.broadcast_to(
                    side_out[side, row : row + 1, :], (8, depth)
                )
        links[level][1]((0, 1, 4, 5, 6, 7))

    def send_sides(level):
        links[level][1]((2, 3))

    def receive_sides(level):
        links[level][2]((2, 3, 4, 5, 6, 7))

    def receive_rows(level):
        links[level][2]((0, 1))

    def tap_sum(parts):
        length, depth = parts.shape[0], parts.shape[1] // 3
        at = lax.broadcasted_iota(jnp.int32, (8, depth), 0)
        before = pltpu.roll(parts[:, 0:depth], 1, axis=0)
        after = pltpu.roll(parts[:, 2 * depth :], length - 1, axis=0)
        before = jnp.concatenate([jnp.where(at == 0, 0.0, before[0:8]), before[8:]], axis=0)
        after = jnp.concatenate(
            [after[: length - 8], jnp.where(at == 7, 0.0, after[length - 8 :])], axis=0
        )
        return before + parts[:, depth : 2 * depth] + after

    def side_terms(level, term, left, right):
        count, _, _, side_in, _ = bufs[level]
        for side, weights in ((0, left), (1, right)):
            lhs = jnp.concatenate(
                [side_in[side, 7 + tap : 7 + tap + count, :] for tap in range(3)], axis=1
            )
            term[side] = dot(lhs.astype(BF16), weights)

    def summed(acc, term, row):
        length, depth = acc.shape[1], acc.shape[2]
        at = lax.broadcasted_iota(jnp.int32, (8, depth), 0)
        head = acc[row, 0:8, :] + jnp.where(at == 0, term[0, pl.ds(row, 1), :], 0.0)
        tail = acc[row, length - 8 : length, :] + jnp.where(
            at == 7, term[1, pl.ds(row, 1), :], 0.0
        )
        return jnp.concatenate([head, acc[row, 8 : length - 8, :], tail], axis=0)

    level_now = jnp.full((1, c1), now_ref[0], F32)
    scale_in = 1.0 / jnp.sqrt(level_now * level_now + 1.0)
    scale_one = scale_in[0:1, 0:1]
    load_small[0].wait()
    noisy_t[...] = jnp.transpose(scale_one * noisy_ref[...])
    mine = noisy_t[pl.ds(first, cols), :]
    load_small[1].wait()
    proj = proj_ref[...]
    load_cond.wait()
    for row in range(height):
        value = cond[row].astype(F32) + mine[:, row : row + 1] * proj
        put_row(0, row, value.astype(BF16))
    pl.semaphore_wait(barrier, greeted)
    send_rows(0)
    send_sides(0)

    def fine_pairs(layer, hp, group):
        lhs = jnp.concatenate(
            [jnp.concatenate([hp[2 * i + j] for j in range(4)], axis=1) for i in group], axis=0
        )
        parts = dot(lhs, wf[layer].reshape(4 * c1, 6 * c1))
        for k, i in enumerate(group):
            for j in range(2):
                acc0[2 * i + j] = tap_sum(
                    parts[k * cols : (k + 1) * cols, 3 * j * c1 : 3 * (j + 1) * c1]
                )

    border = (0, pairs - 1)

    inner = tuple(range(1, pairs - 1))

    def fine_inner(layer, hp):
        for copy in load_fine[layer]:
            copy.wait()
        for at in range(0, len(inner), 2):
            fine_pairs(layer, hp, inner[at : at + 2])

    def fine_sides(layer, level):
        receive_sides(level)
        side_terms(
            level, term0,
            wf[layer, 0:3, :, 0:c1].reshape(3 * c1, c1),
            wf[layer, 0:3, :, 2 * c1 : 3 * c1].reshape(3 * c1, c1),
        )

    pool_at = lax.broadcasted_iota(jnp.int32, (half, 2 * cols), 1)
    pool_to = lax.broadcasted_iota(jnp.int32, (half, 2 * cols), 0)
    pool_at = jnp.where(pool_at >= cols, pool_at - cols, pool_at)
    pool = jnp.where(jnp.right_shift(pool_at, 1) == pool_to, 0.25, 0.0).astype(BF16)

    def first_end(group):
        pooled = []
        for i in group:
            both = []
            for j in range(2):
                row = 2 * i + j
                value = hp0[row + 1].astype(F32) + silu(summed(acc0, term0, row))
                value = value.astype(BF16)
                h1[row] = value
                both.append(value)
            pooled.append(dot(pool, jnp.concatenate(both, axis=0)).astype(BF16))
        lower = dot(jnp.concatenate(pooled, axis=0), down_ref[...]).astype(BF16)
        for k, i in enumerate(group):
            put_row(1, i, lower[k * half : (k + 1) * half])

    fine_inner(0, hp0)
    load_small[2].wait()
    fine_sides(0, 0)
    receive_rows(0)
    fine_pairs(0, hp0, border)
    first_end(border)
    send_rows(1)
    first_end(inner)
    send_sides(1)

    lift_at = lax.broadcasted_iota(jnp.int32, (cols, half), 0)
    lift_to = lax.broadcasted_iota(jnp.int32, (cols, half), 1)
    lift = jnp.where(jnp.right_shift(lift_at, 1) == lift_to, 1.0, 0.0).astype(BF16)

    def coarse_rows(group):
        lhs = jnp.concatenate(
            [jnp.concatenate([hp1[i + j] for j in range(3)], axis=1) for i in group], axis=0
        )
        parts = dot(lhs, wc[...].reshape(3 * c2, 3 * c2))
        for k, i in enumerate(group):
            acc1[i] = tap_sum(parts[k * half : (k + 1) * half])

    def second_start(group):
        wide = []
        for i in group:
            value = hp1[i + 1].astype(F32) + silu(summed(acc1, term1, i))
            wide.append(dot(lift, value.astype(BF16)).astype(BF16))
        lifted = dot(jnp.concatenate(wide, axis=0), up_ref[...])
        for k, i in enumerate(group):
            for j in range(2):
                row = 2 * i + j
                value = h1[row].astype(F32) + lifted[k * cols : (k + 1) * cols]
                put_row(2, row, value.astype(BF16))

    for copy in load_coarse:
        copy.wait()
    load_small[3].wait()
    coarse_rows(inner)
    receive_sides(1)
    side_terms(
        1, term1,
        wc[:, :, 0:c2].reshape(3 * c2, c2),
        wc[:, :, 2 * c2 : 3 * c2].reshape(3 * c2, c2),
    )
    receive_rows(1)
    coarse_rows(border)
    second_start(border)
    send_rows(2)
    second_start(inner)
    send_sides(2)

    load_small[4].wait()
    outp = jnp.broadcast_to(outp_ref[...].astype(F32), (16, c1)).astype(BF16)

    def second_end(group):
        for i in group:
            for j in range(2):
                row = 2 * i + j
                value = hp2[row + 1].astype(F32) + silu(summed(acc0, term0, row))
                total = lax.dot_general(
                    outp, value.astype(BF16), (((1,), (1,)), ((), ())),
                    preferred_element_type=F32,
                )
                net[g, pl.ds(row, 1), :] = total[0:1, :]

    fine_inner(1, hp2)
    fine_sides(1, 2)
    second_end(inner)
    receive_rows(2)
    fine_pairs(1, hp2, border)
    second_end(border)

    shares = []
    for step in range(1, n_rep):
        share = pltpu.make_async_remote_copy(
            src_ref=net.at[g],
            dst_ref=net.at[g],
            send_sem=net_send.at[step - 1],
            recv_sem=net_recv.at[step - 1],
            device_id={"fsdp": lax.rem(f + step, n_rep)},
            device_id_type=MESH,
        )
        share.start()
        shares.append(share)
    for _, _, _, finish in links:
        finish()
    for step in range(1, n_rep):
        owner = place(lax.rem(f + n_rep - step, n_rep), s)
        pltpu.make_async_remote_copy(
            src_ref=net.at[owner],
            dst_ref=net.at[owner],
            send_sem=net_send.at[step - 1],
            recv_sem=net_recv.at[step - 1],
            device_id={"fsdp": lax.rem(f + step, n_rep)},
            device_id_type=MESH,
        ).wait_recv()
    for share in shares:
        share.wait_send()

    load_small[5].wait()

    network = jnp.concatenate([net[k] for k in range(n_rep)], axis=1)
    level_next = jnp.full((1, c1), next_ref[0], F32)
    scale_skip = (1.0 / (level_now * level_now + 1.0))[0:1, 0:1]
    scale_out = (level_now * scale_in)[0:1, 0:1]
    ratio = (level_next / level_now)[0:1, 0:1]
    spread = jnp.sqrt(level_now * level_now - level_next * level_next)[0:1, 0:1]
    noisy = noisy_ref[...]
    denoised = scale_skip * noisy + scale_out * network
    out_ref[...] = denoised + ratio * (noisy - denoised) + spread * draw_ref[...]


def per_device(
    sizes,
    noisy_field, noise_draw, cond_features, sigma_now, sigma_next, field_proj,
    fine_kernels, coarse_kernel, down_proj, up_proj, out_proj,
):
    n_rep = sizes[1]
    height, breadth, c1 = cond_features.shape
    c2 = coarse_kernel.shape[2]
    cols = breadth // n_rep
    pairs, half = height // 2, cols // 2

    def level_bufs(rows, depth):
        return [
            pltpu.VMEM((2, rows, depth), F32),
            pltpu.VMEM((2, rows + 16, depth), F32),
            pltpu.VMEM((4, 8, depth), F32),
        ]

    smem = pl.BlockSpec(memory_space=pltpu.SMEM)
    vmem = pl.BlockSpec(memory_space=pltpu.VMEM)
    hbm = pl.BlockSpec(memory_space=pltpu.HBM)
    return pl.pallas_call(
        functools.partial(kernel, sizes),
        out_shape=jax.ShapeDtypeStruct((height, breadth), F32),
        in_specs=[smem] * 2 + [hbm] * 9,
        out_specs=vmem,
        scratch_shapes=[
            pltpu.VMEM((height, breadth), F32),
            pltpu.VMEM((height, breadth), F32),
            pltpu.VMEM((1, c1), F32),
            pltpu.VMEM((1, c1), BF16),
            pltpu.VMEM((c1, c2), BF16),
            pltpu.VMEM((c2, c1), BF16),
            pltpu.VMEM((height, cols, c1), BF16),
            pltpu.VMEM((2, 4, c1, 6 * c1), BF16),
            pltpu.VMEM((3, c2, 3 * c2), BF16),
            pltpu.VMEM((height + 2, cols, c1), BF16),
            pltpu.VMEM((pairs + 2, half, c2), BF16),
            pltpu.VMEM((height + 2, cols, c1), BF16),
            pltpu.VMEM((height, cols, c1), BF16),
            pltpu.VMEM((breadth, height), F32),
            pltpu.VMEM((height, cols, c1), F32),
            pltpu.VMEM((pairs, half, c2), F32),
            pltpu.VMEM((2, height, c1), F32),
            pltpu.VMEM((2, pairs, c2), F32),
            pltpu.VMEM((n_rep, height, cols), F32),
        ]
        + level_bufs(height, c1)
        + level_bufs(pairs, c2)
        + level_bufs(height, c1)
        + [
            pltpu.SemaphoreType.DMA((22,)),
            pltpu.SemaphoreType.DMA((3, 8)),
            pltpu.SemaphoreType.DMA((3, 8)),
            pltpu.SemaphoreType.DMA((max(n_rep - 1, 1),)),
            pltpu.SemaphoreType.DMA((max(n_rep - 1, 1),)),
        ],
        compiler_params=pltpu.CompilerParams(
            collective_id=0, has_side_effects=True, vmem_limit_bytes=63 * 1024 * 1024
        ),
    )(
        sigma_now, sigma_next, noisy_field, noise_draw,
        field_proj.reshape(1, c1), out_proj.reshape(1, c1), down_proj, up_proj,
        cond_features,
        fine_kernels.reshape(2, 3, 3, c1, c1), coarse_kernel.reshape(3, 3, c2, c2),
    )


def solution(mesh):
    sizes = (mesh.shape["patch"], mesh.shape["fsdp"], mesh.shape["sub"])
    field = P(("groups", "patch"), "sub")
    return jax.shard_map(
        functools.partial(per_device, sizes),
        mesh=mesh,
        in_specs=(field, field, P(("groups", "patch"), "sub", None)) + (P(),) * 8,
        out_specs=field,
        check_vma=False,
    )
```

```python
import functools
import jax
import jax.numpy as jnp
from jax import lax
from jax.experimental import pallas as pl
from jax.experimental.pallas import tpu as pltpu
from jax.sharding import PartitionSpec as P

MESH = pl.DeviceIdType.MESH
BF16 = jnp.bfloat16
F32 = jnp.float32

WAYS = ((-1, 0), (1, 0), (0, -1), (0, 1), (-1, -1), (-1, 1), (1, -1), (1, 1))
BACK = (1, 0, 3, 2, 7, 6, 5, 4)


def silu(v):
    return (0.5 * v) * (1.0 + jnp.tanh(0.5 * v))


def dot(a, b):
    return jnp.dot(a, b, preferred_element_type=F32)


def kernel(
    sizes,
    now_ref, next_ref, noisy_hbm, draw_hbm, proj_hbm, outp_hbm, down_hbm, up_hbm,
    cond_hbm, fine_hbm, coarse_hbm,
    out_ref,
    noisy_ref, draw_ref, proj_ref, outp_ref, down_ref, up_ref,
    cond, wf, wc, hp0, hp1, hp2, h1, noisy_t, acc0, acc1, term0, term1, net,
    side_out0, side_in0, corner_out0,
    side_out1, side_in1, corner_out1,
    side_out2, side_in2, corner_out2,
    load_sem, send_sem, recv_sem, net_send, net_recv,
):
    n_patch, n_rep, n_sub = sizes
    n_part = n_rep * n_sub
    height, cols, c1 = cond.shape
    pairs = height // 2
    half = cols // 2
    c2 = wc.shape[1]

    p = lax.axis_index("patch")
    f = lax.axis_index("fsdp")
    s = lax.axis_index("sub")

    def place(rep, sub):
        return rep + lax.rem(sub, 2) * (n_rep - 1 - 2 * rep)

    g = place(f, s)
    q = s * n_rep + g

    across = []
    for other in (q - 1, q, q + 1):
        other_s = lax.div(other, n_rep)
        across.append((place(other - other_s * n_rep, other_s), other_s))
    inside_p = {-1: p > 0, 1: p < n_patch - 1}
    inside_q = {-1: q > 0, 1: q < n_part - 1}
    devices, inside = [], []
    for dp, dq in WAYS:
        to_f, to_s = across[dq + 1]
        devices.append({"patch": p + dp, "fsdp": to_f, "sub": to_s})
        if dp == 0:
            inside.append(inside_q[dq])
        elif dq == 0:
            inside.append(inside_p[dp])
        else:
            inside.append(jnp.logical_and(inside_p[dp], inside_q[dq]))

    def device(way):
        return devices[way]

    def has(way):
        return inside[way]

    barrier = pltpu.get_barrier_semaphore()
    greeted = n_rep - 1
    for way in range(8):
        there = has(way)

        @pl.when(there)
        def _(way=way):
            pl.semaphore_signal(barrier, inc=1, device_id=device(way), device_id_type=MESH)

        greeted = greeted + there.astype(jnp.int32)
    for step in range(1, n_rep):
        pl.semaphore_signal(
            barrier, inc=1, device_id={"fsdp": lax.rem(f + step, n_rep)}, device_id_type=MESH
        )

    first = pl.multiple_of(g * cols, cols)
    load_cond = pltpu.make_async_copy(cond_hbm.at[:, pl.ds(first, cols), :], cond, load_sem.at[21])
    load_small = [
        pltpu.make_async_copy(src, dst, load_sem.at[k])
        for k, (src, dst) in enumerate(
            (
                (noisy_hbm, noisy_ref),
                (proj_hbm, proj_ref),
                (down_hbm, down_ref),
                (up_hbm, up_ref),
                (outp_hbm, outp_ref),
                (draw_hbm, draw_ref),
            )
        )
    ]
    load_small[0].start()
    load_small[1].start()
    load_cond.start()
    for tap in range(3):
        upper, lower = 2 * tap * c1, (2 * tap + 1) * c1
        wf[:, 3:4, :, upper : upper + c1] = jnp.zeros((2, 1, c1, c1), BF16)
        wf[:, 0:1, :, lower : lower + c1] = jnp.zeros((2, 1, c1, c1), BF16)
    load_fine = [
        [
            pltpu.make_async_copy(
                fine_hbm.at[layer, :, tap],
                wf.at[layer, low : low + 3, :, (2 * tap + low) * c1 : (2 * tap + low + 1) * c1],
                load_sem.at[6 + 6 * layer + 3 * low + tap],
            )
            for low in range(2)
            for tap in range(3)
        ]
        for layer in range(2)
    ]
    load_coarse = [
        pltpu.make_async_copy(
            coarse_hbm.at[:, tap], wc.at[:, :, tap * c2 : (tap + 1) * c2], load_sem.at[18 + tap]
        )
        for tap in range(3)
    ]
    for copy in load_fine[0] + [load_small[2]] + load_coarse + [load_small[3]] + load_fine[1]:
        copy.start()
    load_small[4].start()
    load_small[5].start()

    def copies(level, count, hp, side_out, side_in, corner_out):
        own = pl.ds(8, count)
        above = pl.ds(0, 8)
        below = pl.ds(count + 8, 8)
        routes = [
            (hp.at[1], hp.at[count + 1]),
            (hp.at[count], hp.at[0]),
            (side_out.at[0], side_in.at[1, own, :]),
            (side_out.at[1], side_in.at[0, own, :]),
            (corner_out.at[0], side_in.at[1, below, :]),
            (corner_out.at[1], side_in.at[0, below, :]),
            (corner_out.at[2], side_in.at[1, above, :]),
            (corner_out.at[3], side_in.at[0, above, :]),
        ]

        def copy(way):
            return pltpu.make_async_remote_copy(
                src_ref=routes[way][0],
                dst_ref=routes[way][1],
                send_sem=send_sem.at[level, way],
                recv_sem=recv_sem.at[level, way],
                device_id=device(way),
                device_id_type=MESH,
            )

        def clear():
            for way in range(8):
                @pl.when(jnp.logical_not(has(BACK[way])))
                def _(way=way):
                    into = routes[way][1]
                    into[...] = jnp.zeros(into.shape, into.dtype)

        def send(ways):
            for way in ways:
                @pl.when(has(way))
                def _(way=way):
                    copy(way).start()

        def receive(ways):
            for way in ways:
                @pl.when(has(BACK[way]))
                def _(way=way):
                    copy(way).wait_recv()

        def finish():
            for way in range(8):
                @pl.when(has(way))
                def _(way=way):
                    copy(way).wait_send()

        return clear, send, receive, finish

    bufs = (
        (height, hp0, side_out0, side_in0, corner_out0),
        (pairs, hp1, side_out1, side_in1, corner_out1),
        (height, hp2, side_out2, side_in2, corner_out2),
    )
    links = [copies(level, *bufs[level]) for level in range(3)]
    for clear, _, _, _ in links:
        clear()

    def put_row(level, row, value):
        _, hp, side_out, _, _ = bufs[level]
        length = value.shape[0]
        hp[row + 1] = value
        side_out[0, pl.ds(row, 1), :] = value[0:8, :].astype(F32)[0:1, :]
        side_out[1, pl.ds(row, 1), :] = value[length - 16 :, :].astype(F32)[15:16, :]

    def send_rows(level):
        count, _, side_out, _, corner_out = bufs[level]
        depth = side_out.shape[2]
        for end, row in ((0, 0), (1, count - 1)):
            for side in range(2):
                corner_out[2 * end + side] = jnp.broadcast_to(
                    side_out[side, row : row + 1, :], (8, depth)
                )
        links[level][1]((0, 1, 4, 5, 6, 7))

    def send_sides(level):
        links[level][1]((2, 3))

    def receive_sides(level):
        links[level][2]((2, 3, 4, 5, 6, 7))

    def receive_rows(level):
        links[level][2]((0, 1))

    def tap_sum(before, centre, after):
        length, depth = centre.shape
        at = lax.broadcasted_iota(jnp.int32, (8, depth), 0)
        before = pltpu.roll(before, 1, axis=0)
        after = pltpu.roll(after, length - 1, axis=0)
        before = jnp.concatenate([jnp.where(at == 0, 0.0, before[0:8]), before[8:]], axis=0)
        after = jnp.concatenate(
            [after[: length - 8], jnp.where(at == 7, 0.0, after[length - 8 :])], axis=0
        )
        return before + centre + after

    def side_terms(level, term, left, right):
        count, _, _, side_in, _ = bufs[level]
        for side, weights in ((0, left), (1, right)):
            lhs = jnp.concatenate(
                [side_in[side, 7 + tap : 7 + tap + count, :] for tap in range(3)], axis=1
            )
            term[side] = dot(lhs.astype(BF16), weights)

    def summed(acc, term, row):
        length, depth = acc.shape[1], acc.shape[2]
        at = lax.broadcasted_iota(jnp.int32, (8, depth), 0)
        head = acc[row, 0:8, :] + jnp.where(at == 0, term[0, pl.ds(row, 1), :], 0.0)
        tail = acc[row, length - 8 : length, :] + jnp.where(
            at == 7, term[1, pl.ds(row, 1), :], 0.0
        )
        return jnp.concatenate([head, acc[row, 8 : length - 8, :], tail], axis=0)

    level_now = jnp.full((1, c1), now_ref[0], F32)
    scale_in = 1.0 / jnp.sqrt(level_now * level_now + 1.0)
    scale_one = scale_in[0:1, 0:1]
    load_small[0].wait()
    noisy_t[...] = jnp.transpose(scale_one * noisy_ref[...])
    mine = noisy_t[pl.ds(first, cols), :]
    load_small[1].wait()
    proj = proj_ref[...]
    load_cond.wait()
    for row in range(height):
        value = cond[row].astype(F32) + mine[:, row : row + 1] * proj
        put_row(0, row, value.astype(BF16))
    pl.semaphore_wait(barrier, greeted)
    send_rows(0)
    send_sides(0)

    def fine_pairs(layer, hp, group):
        lhs = jnp.concatenate(
            [jnp.concatenate([hp[2 * i + j] for j in range(4)], axis=1) for i in group], axis=0
        )
        parts = [
            dot(lhs, wf[layer, :, :, 2 * tap * c1 : 2 * (tap + 1) * c1].reshape(4 * c1, 2 * c1))
            for tap in range(3)
        ]
        for k, i in enumerate(group):
            for j in range(2):
                acc0[2 * i + j] = tap_sum(
                    *(p[k * cols : (k + 1) * cols, j * c1 : (j + 1) * c1] for p in parts)
                )

    border = (0, pairs - 1)

    inner = tuple(range(1, pairs - 1))

    def fine_inner(layer, hp):
        for copy in load_fine[layer]:
            copy.wait()
        fine_pairs(layer, hp, inner)

    def fine_sides(layer, level):
        receive_sides(level)
        side_terms(
            level, term0,
            wf[layer, 0:3, :, 0:c1].reshape(3 * c1, c1),
            wf[layer, 0:3, :, 4 * c1 : 5 * c1].reshape(3 * c1, c1),
        )

    pool_at = lax.broadcasted_iota(jnp.int32, (half, 2 * cols), 1)
    pool_to = lax.broadcasted_iota(jnp.int32, (half, 2 * cols), 0)
    pool_at = jnp.where(pool_at >= cols, pool_at - cols, pool_at)
    pool = jnp.where(jnp.right_shift(pool_at, 1) == pool_to, 0.25, 0.0).astype(BF16)

    def first_end(group):
        pooled = []
        for i in group:
            both = []
            for j in range(2):
                row = 2 * i + j
                value = hp0[row + 1].astype(F32) + silu(summed(acc0, term0, row))
                value = value.astype(BF16)
                h1[row] = value
                both.append(value)
            pooled.append(dot(pool, jnp.concatenate(both, axis=0)).astype(BF16))
        lower = dot(jnp.concatenate(pooled, axis=0), down_ref[...]).astype(BF16)
        for k, i in enumerate(group):
            put_row(1, i, lower[k * half : (k + 1) * half])

    fine_inner(0, hp0)
    load_small[2].wait()
    fine_sides(0, 0)
    receive_rows(0)
    fine_pairs(0, hp0, border)
    first_end(border)
    send_rows(1)
    first_end(inner)
    send_sides(1)

    lift_at = lax.broadcasted_iota(jnp.int32, (cols, half), 0)
    lift_to = lax.broadcasted_iota(jnp.int32, (cols, half), 1)
    lift = jnp.where(jnp.right_shift(lift_at, 1) == lift_to, 1.0, 0.0).astype(BF16)

    def coarse_rows(group):
        lhs = jnp.concatenate(
            [jnp.concatenate([hp1[i + j] for j in range(3)], axis=1) for i in group], axis=0
        )
        parts = dot(lhs, wc[...].reshape(3 * c2, 3 * c2))
        for k, i in enumerate(group):
            acc1[i] = tap_sum(
                *(parts[k * half : (k + 1) * half, t * c2 : (t + 1) * c2] for t in range(3))
            )

    def second_start(group):
        wide = []
        for i in group:
            value = hp1[i + 1].astype(F32) + silu(summed(acc1, term1, i))
            wide.append(dot(lift, value.astype(BF16)).astype(BF16))
        lifted = dot(jnp.concatenate(wide, axis=0), up_ref[...])
        for k, i in enumerate(group):
            for j in range(2):
                row = 2 * i + j
                value = h1[row].astype(F32) + lifted[k * cols : (k + 1) * cols]
                put_row(2, row, value.astype(BF16))

    for copy in load_coarse:
        copy.wait()
    load_small[3].wait()
    coarse_rows(inner)
    receive_sides(1)
    side_terms(
        1, term1,
        wc[:, :, 0:c2].reshape(3 * c2, c2),
        wc[:, :, 2 * c2 : 3 * c2].reshape(3 * c2, c2),
    )
    receive_rows(1)
    coarse_rows(border)
    second_start(border)
    send_rows(2)
    second_start(inner)
    send_sides(2)

    load_small[4].wait()
    outp = jnp.broadcast_to(outp_ref[...].astype(F32), (16, c1)).astype(BF16)

    def second_end(group):
        for i in group:
            for j in range(2):
                row = 2 * i + j
                value = hp2[row + 1].astype(F32) + silu(summed(acc0, term0, row))
                total = lax.dot_general(
                    outp, value.astype(BF16), (((1,), (1,)), ((), ())),
                    preferred_element_type=F32,
                )
                net[g, pl.ds(row, 1), :] = total[0:1, :]

    fine_inner(1, hp2)
    fine_sides(1, 2)
    second_end(inner)
    receive_rows(2)
    fine_pairs(1, hp2, border)
    second_end(border)

    shares = []
    for step in range(1, n_rep):
        share = pltpu.make_async_remote_copy(
            src_ref=net.at[g],
            dst_ref=net.at[g],
            send_sem=net_send.at[step - 1],
            recv_sem=net_recv.at[step - 1],
            device_id={"fsdp": lax.rem(f + step, n_rep)},
            device_id_type=MESH,
        )
        share.start()
        shares.append(share)
    for _, _, _, finish in links:
        finish()
    for step in range(1, n_rep):
        owner = place(lax.rem(f + n_rep - step, n_rep), s)
        pltpu.make_async_remote_copy(
            src_ref=net.at[owner],
            dst_ref=net.at[owner],
            send_sem=net_send.at[step - 1],
            recv_sem=net_recv.at[step - 1],
            device_id={"fsdp": lax.rem(f + step, n_rep)},
            device_id_type=MESH,
        ).wait_recv()
    for share in shares:
        share.wait_send()

    load_small[5].wait()

    network = jnp.concatenate([net[k] for k in range(n_rep)], axis=1)
    level_next = jnp.full((1, c1), next_ref[0], F32)
    scale_skip = (1.0 / (level_now * level_now + 1.0))[0:1, 0:1]
    scale_out = (level_now * scale_in)[0:1, 0:1]
    ratio = (level_next / level_now)[0:1, 0:1]
    spread = jnp.sqrt(level_now * level_now - level_next * level_next)[0:1, 0:1]
    noisy = noisy_ref[...]
    denoised = scale_skip * noisy + scale_out * network
    out_ref[...] = denoised + ratio * (noisy - denoised) + spread * draw_ref[...]


def per_device(
    sizes,
    noisy_field, noise_draw, cond_features, sigma_now, sigma_next, field_proj,
    fine_kernels, coarse_kernel, down_proj, up_proj, out_proj,
):
    n_rep = sizes[1]
    height, breadth, c1 = cond_features.shape
    c2 = coarse_kernel.shape[2]
    cols = breadth // n_rep
    pairs, half = height // 2, cols // 2

    def level_bufs(rows, depth):
        return [
            pltpu.VMEM((2, rows, depth), F32),
            pltpu.VMEM((2, rows + 16, depth), F32),
            pltpu.VMEM((4, 8, depth), F32),
        ]

    smem = pl.BlockSpec(memory_space=pltpu.SMEM)
    vmem = pl.BlockSpec(memory_space=pltpu.VMEM)
    hbm = pl.BlockSpec(memory_space=pltpu.HBM)
    return pl.pallas_call(
        functools.partial(kernel, sizes),
        out_shape=jax.ShapeDtypeStruct((height, breadth), F32),
        in_specs=[smem] * 2 + [hbm] * 9,
        out_specs=vmem,
        scratch_shapes=[
            pltpu.VMEM((height, breadth), F32),
            pltpu.VMEM((height, breadth), F32),
            pltpu.VMEM((1, c1), F32),
            pltpu.VMEM((1, c1), BF16),
            pltpu.VMEM((c1, c2), BF16),
            pltpu.VMEM((c2, c1), BF16),
            pltpu.VMEM((height, cols, c1), BF16),
            pltpu.VMEM((2, 4, c1, 6 * c1), BF16),
            pltpu.VMEM((3, c2, 3 * c2), BF16),
            pltpu.VMEM((height + 2, cols, c1), BF16),
            pltpu.VMEM((pairs + 2, half, c2), BF16),
            pltpu.VMEM((height + 2, cols, c1), BF16),
            pltpu.VMEM((height, cols, c1), BF16),
            pltpu.VMEM((breadth, height), F32),
            pltpu.VMEM((height, cols, c1), F32),
            pltpu.VMEM((pairs, half, c2), F32),
            pltpu.VMEM((2, height, c1), F32),
            pltpu.VMEM((2, pairs, c2), F32),
            pltpu.VMEM((n_rep, height, cols), F32),
        ]
        + level_bufs(height, c1)
        + level_bufs(pairs, c2)
        + level_bufs(height, c1)
        + [
            pltpu.SemaphoreType.DMA((22,)),
            pltpu.SemaphoreType.DMA((3, 8)),
            pltpu.SemaphoreType.DMA((3, 8)),
            pltpu.SemaphoreType.DMA((max(n_rep - 1, 1),)),
            pltpu.SemaphoreType.DMA((max(n_rep - 1, 1),)),
        ],
        compiler_params=pltpu.CompilerParams(
            collective_id=0, has_side_effects=True, vmem_limit_bytes=63 * 1024 * 1024
        ),
    )(
        sigma_now, sigma_next, noisy_field, noise_draw,
        field_proj.reshape(1, c1), out_proj.reshape(1, c1), down_proj, up_proj,
        cond_features,
        fine_kernels.reshape(2, 3, 3, c1, c1), coarse_kernel.reshape(3, 3, c2, c2),
    )


def solution(mesh):
    sizes = (mesh.shape["patch"], mesh.shape["fsdp"], mesh.shape["sub"])
    field = P(("groups", "patch"), "sub")
    return jax.shard_map(
        functools.partial(per_device, sizes),
        mesh=mesh,
        in_specs=(field, field, P(("groups", "patch"), "sub", None)) + (P(),) * 8,
        out_specs=field,
        check_vma=False,
    )
```

```python
import functools
import jax
import jax.numpy as jnp
from jax import lax
from jax.experimental import pallas as pl
from jax.experimental.pallas import tpu as pltpu
from jax.sharding import PartitionSpec as P

MESH = pl.DeviceIdType.MESH
BF16 = jnp.bfloat16
F32 = jnp.float32

WAYS = ((-1, 0), (1, 0), (0, -1), (0, 1), (-1, -1), (-1, 1), (1, -1), (1, 1))
BACK = (1, 0, 3, 2, 7, 6, 5, 4)


def silu(v):
    return (0.5 * v) * (1.0 + jnp.tanh(0.5 * v))


def dot(a, b):
    return jnp.dot(a, b, preferred_element_type=F32)


def kernel(
    sizes,
    now_ref, next_ref, noisy_hbm, draw_hbm, proj_hbm, outp_hbm, down_hbm, up_hbm,
    cond_hbm, fine_hbm, coarse_hbm,
    out_ref,
    noisy_ref, draw_ref, proj_ref, outp_ref, down_ref, up_ref,
    cond, wf, wc, hp0, hp1, hp2, h1, noisy_t, acc0, acc1, term0, term1, net,
    side_out0, side_in0, corner_out0,
    side_out1, side_in1, corner_out1,
    side_out2, side_in2, corner_out2,
    load_sem, send_sem, recv_sem, net_send, net_recv,
):
    n_patch, n_rep, n_sub = sizes
    n_part = n_rep * n_sub
    height, cols, c1 = cond.shape
    pairs = height // 2
    half = cols // 2
    c2 = wc.shape[1]

    p = lax.axis_index("patch")
    f = lax.axis_index("fsdp")
    s = lax.axis_index("sub")

    def place(rep, sub):
        return rep + lax.rem(sub, 2) * (n_rep - 1 - 2 * rep)

    g = place(f, s)
    q = s * n_rep + g

    across = []
    for other in (q - 1, q, q + 1):
        other_s = lax.div(other, n_rep)
        across.append((place(other - other_s * n_rep, other_s), other_s))
    inside_p = {-1: p > 0, 1: p < n_patch - 1}
    inside_q = {-1: q > 0, 1: q < n_part - 1}
    devices, inside = [], []
    for dp, dq in WAYS:
        to_f, to_s = across[dq + 1]
        devices.append({"patch": p + dp, "fsdp": to_f, "sub": to_s})
        if dp == 0:
            inside.append(inside_q[dq])
        elif dq == 0:
            inside.append(inside_p[dp])
        else:
            inside.append(jnp.logical_and(inside_p[dp], inside_q[dq]))

    def device(way):
        return devices[way]

    def has(way):
        return inside[way]

    barrier = pltpu.get_barrier_semaphore()
    greeted = n_rep - 1
    for way in range(8):
        there = has(way)

        @pl.when(there)
        def _(way=way):
            pl.semaphore_signal(barrier, inc=1, device_id=device(way), device_id_type=MESH)

        greeted = greeted + there.astype(jnp.int32)
    for step in range(1, n_rep):
        pl.semaphore_signal(
            barrier, inc=1, device_id={"fsdp": lax.rem(f + step, n_rep)}, device_id_type=MESH
        )

    first = pl.multiple_of(g * cols, cols)
    load_cond = pltpu.make_async_copy(cond_hbm.at[:, pl.ds(first, cols), :], cond, load_sem.at[21])
    load_small = [
        pltpu.make_async_copy(src, dst, load_sem.at[k])
        for k, (src, dst) in enumerate(
            (
                (noisy_hbm, noisy_ref),
                (proj_hbm, proj_ref),
                (down_hbm, down_ref),
                (up_hbm, up_ref),
                (outp_hbm, outp_ref),
                (draw_hbm, draw_ref),
            )
        )
    ]
    load_small[0].start()
    load_small[1].start()
    load_cond.start()
    wf[:, 3:4, :, 0 : 3 * c1] = jnp.zeros((2, 1, c1, 3 * c1), BF16)
    wf[:, 0:1, :, 3 * c1 :] = jnp.zeros((2, 1, c1, 3 * c1), BF16)
    load_fine = [
        [
            pltpu.make_async_copy(
                fine_hbm.at[layer, :, tap],
                wf.at[layer, low : low + 3, :, (3 * low + tap) * c1 : (3 * low + tap + 1) * c1],
                load_sem.at[6 + 6 * layer + 3 * low + tap],
            )
            for low in range(2)
            for tap in range(3)
        ]
        for layer in range(2)
    ]
    load_coarse = [
        pltpu.make_async_copy(
            coarse_hbm.at[:, tap], wc.at[:, :, tap * c2 : (tap + 1) * c2], load_sem.at[18 + tap]
        )
        for tap in range(3)
    ]
    for copy in load_fine[0] + [load_small[2]] + load_coarse + [load_small[3]] + load_fine[1]:
        copy.start()
    load_small[4].start()
    load_small[5].start()

    def copies(level, count, hp, side_out, side_in, corner_out):
        own = pl.ds(8, count)
        above = pl.ds(0, 8)
        below = pl.ds(count + 8, 8)
        routes = [
            (hp.at[1], hp.at[count + 1]),
            (hp.at[count], hp.at[0]),
            (side_out.at[0], side_in.at[1, own, :]),
            (side_out.at[1], side_in.at[0, own, :]),
            (corner_out.at[0], side_in.at[1, below, :]),
            (corner_out.at[1], side_in.at[0, below, :]),
            (corner_out.at[2], side_in.at[1, above, :]),
            (corner_out.at[3], side_in.at[0, above, :]),
        ]

        def copy(way):
            return pltpu.make_async_remote_copy(
                src_ref=routes[way][0],
                dst_ref=routes[way][1],
                send_sem=send_sem.at[level, way],
                recv_sem=recv_sem.at[level, way],
                device_id=device(way),
                device_id_type=MESH,
            )

        def clear():
            for way in range(8):
                @pl.when(jnp.logical_not(has(BACK[way])))
                def _(way=way):
                    into = routes[way][1]
                    into[...] = jnp.zeros(into.shape, into.dtype)

        def send(ways):
            for way in ways:
                @pl.when(has(way))
                def _(way=way):
                    copy(way).start()

        def receive(ways):
            for way in ways:
                @pl.when(has(BACK[way]))
                def _(way=way):
                    copy(way).wait_recv()

        def finish():
            for way in range(8):
                @pl.when(has(way))
                def _(way=way):
                    copy(way).wait_send()

        return clear, send, receive, finish

    bufs = (
        (height, hp0, side_out0, side_in0, corner_out0),
        (pairs, hp1, side_out1, side_in1, corner_out1),
        (height, hp2, side_out2, side_in2, corner_out2),
    )
    links = [copies(level, *bufs[level]) for level in range(3)]
    for clear, _, _, _ in links:
        clear()

    def put_row(level, row, value):
        _, hp, side_out, _, _ = bufs[level]
        length = value.shape[0]
        hp[row + 1] = value
        side_out[0, pl.ds(row, 1), :] = value[0:8, :].astype(F32)[0:1, :]
        side_out[1, pl.ds(row, 1), :] = value[length - 16 :, :].astype(F32)[15:16, :]

    def send_rows(level):
        count, _, side_out, _, corner_out = bufs[level]
        depth = side_out.shape[2]
        for end, row in ((0, 0), (1, count - 1)):
            for side in range(2):
                corner_out[2 * end + side] = jnp.broadcast_to(
                    side_out[side, row : row + 1, :], (8, depth)
                )
        links[level][1]((0, 1, 4, 5, 6, 7))

    def send_sides(level):
        links[level][1]((2, 3))

    def receive_sides(level):
        links[level][2]((2, 3, 4, 5, 6, 7))

    def receive_rows(level):
        links[level][2]((0, 1))

    def tap_sum(parts):
        length, depth = parts.shape[0], parts.shape[1] // 3
        at = lax.broadcasted_iota(jnp.int32, (8, depth), 0)
        before = pltpu.roll(parts[:, 0:depth], 1, axis=0)
        after = pltpu.roll(parts[:, 2 * depth :], length - 1, axis=0)
        before = jnp.concatenate([jnp.where(at == 0, 0.0, before[0:8]), before[8:]], axis=0)
        after = jnp.concatenate(
            [after[: length - 8], jnp.where(at == 7, 0.0, after[length - 8 :])], axis=0
        )
        return before + parts[:, depth : 2 * depth] + after

    def side_terms(level, term, left, right):
        count, _, _, side_in, _ = bufs[level]
        for side, weights in ((0, left), (1, right)):
            lhs = jnp.concatenate(
                [side_in[side, 7 + tap : 7 + tap + count, :] for tap in range(3)], axis=1
            )
            term[side] = dot(lhs.astype(BF16), weights)

    def summed(acc, term, row):
        length, depth = acc.shape[1], acc.shape[2]
        at = lax.broadcasted_iota(jnp.int32, (8, depth), 0)
        head = acc[row, 0:8, :] + jnp.where(at == 0, term[0, pl.ds(row, 1), :], 0.0)
        tail = acc[row, length - 8 : length, :] + jnp.where(
            at == 7, term[1, pl.ds(row, 1), :], 0.0
        )
        return jnp.concatenate([head, acc[row, 8 : length - 8, :], tail], axis=0)

    level_now = jnp.full((1, c1), now_ref[0], F32)
    scale_in = 1.0 / jnp.sqrt(level_now * level_now + 1.0)
    scale_one = scale_in[0:1, 0:1]
    load_small[0].wait()
    noisy_t[...] = jnp.transpose(scale_one * noisy_ref[...])
    mine = noisy_t[pl.ds(first, cols), :]
    load_small[1].wait()
    proj = proj_ref[...]
    load_cond.wait()
    def first_rows(rows):
        for row in rows:
            value = cond[row].astype(F32) + mine[:, row : row + 1] * proj
            put_row(0, row, value.astype(BF16))

    first_rows((0, height - 1))
    pl.semaphore_wait(barrier, greeted)
    send_rows(0)
    first_rows(range(1, height - 1))
    send_sides(0)

    def fine_pairs(layer, hp, group):
        lhs = jnp.concatenate(
            [jnp.concatenate([hp[2 * i + j] for j in range(4)], axis=1) for i in group], axis=0
        )
        parts = dot(lhs, wf[layer].reshape(4 * c1, 6 * c1))
        for k, i in enumerate(group):
            for j in range(2):
                acc0[2 * i + j] = tap_sum(
                    parts[k * cols : (k + 1) * cols, 3 * j * c1 : 3 * (j + 1) * c1]
                )

    border = (0, pairs - 1)

    inner = tuple(range(1, pairs - 1))

    def fine_inner(layer, hp):
        for copy in load_fine[layer]:
            copy.wait()
        for at in range(0, len(inner), 2):
            fine_pairs(layer, hp, inner[at : at + 2])

    def fine_sides(layer, level):
        receive_sides(level)
        side_terms(
            level, term0,
            wf[layer, 0:3, :, 0:c1].reshape(3 * c1, c1),
            wf[layer, 0:3, :, 2 * c1 : 3 * c1].reshape(3 * c1, c1),
        )

    pool_at = lax.broadcasted_iota(jnp.int32, (half, 2 * cols), 1)
    pool_to = lax.broadcasted_iota(jnp.int32, (half, 2 * cols), 0)
    pool_at = jnp.where(pool_at >= cols, pool_at - cols, pool_at)
    pool = jnp.where(jnp.right_shift(pool_at, 1) == pool_to, 0.25, 0.0).astype(BF16)

    def first_end(group):
        pooled = []
        for i in group:
            both = []
            for j in range(2):
                row = 2 * i + j
                value = hp0[row + 1].astype(F32) + silu(summed(acc0, term0, row))
                value = value.astype(BF16)
                h1[row] = value
                both.append(value)
            pooled.append(dot(pool, jnp.concatenate(both, axis=0)).astype(BF16))
        lower = dot(jnp.concatenate(pooled, axis=0), down_ref[...]).astype(BF16)
        for k, i in enumerate(group):
            put_row(1, i, lower[k * half : (k + 1) * half])

    fine_inner(0, hp0)
    load_small[2].wait()
    fine_sides(0, 0)
    receive_rows(0)
    fine_pairs(0, hp0, border)
    first_end(border)
    send_rows(1)
    first_end(inner)
    send_sides(1)

    lift_at = lax.broadcasted_iota(jnp.int32, (cols, half), 0)
    lift_to = lax.broadcasted_iota(jnp.int32, (cols, half), 1)
    lift = jnp.where(jnp.right_shift(lift_at, 1) == lift_to, 1.0, 0.0).astype(BF16)

    def coarse_rows(group):
        lhs = jnp.concatenate(
            [jnp.concatenate([hp1[i + j] for j in range(3)], axis=1) for i in group], axis=0
        )
        parts = dot(lhs, wc[...].reshape(3 * c2, 3 * c2))
        for k, i in enumerate(group):
            acc1[i] = tap_sum(parts[k * half : (k + 1) * half])

    def second_start(group):
        wide = []
        for i in group:
            value = hp1[i + 1].astype(F32) + silu(summed(acc1, term1, i))
            wide.append(dot(lift, value.astype(BF16)).astype(BF16))
        lifted = dot(jnp.concatenate(wide, axis=0), up_ref[...])
        for k, i in enumerate(group):
            for j in range(2):
                row = 2 * i + j
                value = h1[row].astype(F32) + lifted[k * cols : (k + 1) * cols]
                put_row(2, row, value.astype(BF16))

    for copy in load_coarse:
        copy.wait()
    load_small[3].wait()
    coarse_rows(inner)
    receive_sides(1)
    side_terms(
        1, term1,
        wc[:, :, 0:c2].reshape(3 * c2, c2),
        wc[:, :, 2 * c2 : 3 * c2].reshape(3 * c2, c2),
    )
    receive_rows(1)
    coarse_rows(border)
    second_start(border)
    send_rows(2)
    second_start(inner)
    send_sides(2)

    load_small[4].wait()
    outp = jnp.broadcast_to(outp_ref[...].astype(F32), (16, c1)).astype(BF16)

    def second_end(group):
        for i in group:
            for j in range(2):
                row = 2 * i + j
                value = hp2[row + 1].astype(F32) + silu(summed(acc0, term0, row))
                total = lax.dot_general(
                    outp, value.astype(BF16), (((1,), (1,)), ((), ())),
                    preferred_element_type=F32,
                )
                net[g, pl.ds(row, 1), :] = total[0:1, :]

    fine_inner(1, hp2)
    fine_sides(1, 2)
    second_end(inner)
    receive_rows(2)
    fine_pairs(1, hp2, border)
    second_end(border)

    shares = []
    for step in range(1, n_rep):
        share = pltpu.make_async_remote_copy(
            src_ref=net.at[g],
            dst_ref=net.at[g],
            send_sem=net_send.at[step - 1],
            recv_sem=net_recv.at[step - 1],
            device_id={"fsdp": lax.rem(f + step, n_rep)},
            device_id_type=MESH,
        )
        share.start()
        shares.append(share)
    for _, _, _, finish in links:
        finish()
    for step in range(1, n_rep):
        owner = place(lax.rem(f + n_rep - step, n_rep), s)
        pltpu.make_async_remote_copy(
            src_ref=net.at[owner],
            dst_ref=net.at[owner],
            send_sem=net_send.at[step - 1],
            recv_sem=net_recv.at[step - 1],
            device_id={"fsdp": lax.rem(f + step, n_rep)},
            device_id_type=MESH,
        ).wait_recv()
    for share in shares:
        share.wait_send()

    load_small[5].wait()

    network = jnp.concatenate([net[k] for k in range(n_rep)], axis=1)
    level_next = jnp.full((1, c1), next_ref[0], F32)
    scale_skip = (1.0 / (level_now * level_now + 1.0))[0:1, 0:1]
    scale_out = (level_now * scale_in)[0:1, 0:1]
    ratio = (level_next / level_now)[0:1, 0:1]
    spread = jnp.sqrt(level_now * level_now - level_next * level_next)[0:1, 0:1]
    noisy = noisy_ref[...]
    denoised = scale_skip * noisy + scale_out * network
    out_ref[...] = denoised + ratio * (noisy - denoised) + spread * draw_ref[...]


def per_device(
    sizes,
    noisy_field, noise_draw, cond_features, sigma_now, sigma_next, field_proj,
    fine_kernels, coarse_kernel, down_proj, up_proj, out_proj,
):
    n_rep = sizes[1]
    height, breadth, c1 = cond_features.shape
    c2 = coarse_kernel.shape[2]
    cols = breadth // n_rep
    pairs, half = height // 2, cols // 2

    def level_bufs(rows, depth):
        return [
            pltpu.VMEM((2, rows, depth), F32),
            pltpu.VMEM((2, rows + 16, depth), F32),
            pltpu.VMEM((4, 8, depth), F32),
        ]

    smem = pl.BlockSpec(memory_space=pltpu.SMEM)
    vmem = pl.BlockSpec(memory_space=pltpu.VMEM)
    hbm = pl.BlockSpec(memory_space=pltpu.HBM)
    return pl.pallas_call(
        functools.partial(kernel, sizes),
        out_shape=jax.ShapeDtypeStruct((height, breadth), F32),
        in_specs=[smem] * 2 + [hbm] * 9,
        out_specs=vmem,
        scratch_shapes=[
            pltpu.VMEM((height, breadth), F32),
            pltpu.VMEM((height, breadth), F32),
            pltpu.VMEM((1, c1), F32),
            pltpu.VMEM((1, c1), BF16),
            pltpu.VMEM((c1, c2), BF16),
            pltpu.VMEM((c2, c1), BF16),
            pltpu.VMEM((height, cols, c1), BF16),
            pltpu.VMEM((2, 4, c1, 6 * c1), BF16),
            pltpu.VMEM((3, c2, 3 * c2), BF16),
            pltpu.VMEM((height + 2, cols, c1), BF16),
            pltpu.VMEM((pairs + 2, half, c2), BF16),
            pltpu.VMEM((height + 2, cols, c1), BF16),
            pltpu.VMEM((height, cols, c1), BF16),
            pltpu.VMEM((breadth, height), F32),
            pltpu.VMEM((height, cols, c1), F32),
            pltpu.VMEM((pairs, half, c2), F32),
            pltpu.VMEM((2, height, c1), F32),
            pltpu.VMEM((2, pairs, c2), F32),
            pltpu.VMEM((n_rep, height, cols), F32),
        ]
        + level_bufs(height, c1)
        + level_bufs(pairs, c2)
        + level_bufs(height, c1)
        + [
            pltpu.SemaphoreType.DMA((22,)),
            pltpu.SemaphoreType.DMA((3, 8)),
            pltpu.SemaphoreType.DMA((3, 8)),
            pltpu.SemaphoreType.DMA((max(n_rep - 1, 1),)),
            pltpu.SemaphoreType.DMA((max(n_rep - 1, 1),)),
        ],
        compiler_params=pltpu.CompilerParams(
            collective_id=0, has_side_effects=True, vmem_limit_bytes=63 * 1024 * 1024
        ),
    )(
        sigma_now, sigma_next, noisy_field, noise_draw,
        field_proj.reshape(1, c1), out_proj.reshape(1, c1), down_proj, up_proj,
        cond_features,
        fine_kernels.reshape(2, 3, 3, c1, c1), coarse_kernel.reshape(3, 3, c2, c2),
    )


def solution(mesh):
    sizes = (mesh.shape["patch"], mesh.shape["fsdp"], mesh.shape["sub"])
    field = P(("groups", "patch"), "sub")
    return jax.shard_map(
        functools.partial(per_device, sizes),
        mesh=mesh,
        in_specs=(field, field, P(("groups", "patch"), "sub", None)) + (P(),) * 8,
        out_specs=field,
        check_vma=False,
    )
```
